256 devices in a mesh: dp: 32 (over x, z), table: 8 (over y, core).
Axes of the slice: x: 4, y: 4, z: 8, core: 2. Of those that a mesh axis runs over, the one named last changes fastest.
Arguments:
- embedding_table: bfloat16 [32768, 512], P('table'), may hold values from -6 to 6
- served_ids: int32 [32, 8, 8, 64], P('dp', 'table'), may hold values from 0 to 4095, as said below
- event_slot: int32 [32, 8, 16, 128], P('dp', 'table'), may hold values from 0 to 511
- block_fill: int32 [32, 8, 16], P('dp', 'table'), may hold values from 0 to 128, as said below
- destination: int32 [32, 8, 16], P('dp', 'table'), may hold values from 0 to 31, as said below
- target: bfloat16 [32, 8, 16, 128, 512], P('dp', 'table'), may hold values from -1.5 to 1.5
- w_in: bfloat16 [512, 1536], replicated, may hold values from -0.25 to 0.25
- w_out: bfloat16 [512, 512], replicated, may hold values from -0.25 to 0.25
- gain_in: float32 [512], replicated, may hold values from 0.1 to 1.9
- gain_out: float32 [512], replicated, may hold values from 0.1 to 1.9
Outputs:
- block_summary: bfloat16 [32, 8, 8, 512], P('dp', 'table')
- row_gradient: float32 [8, 4096, 512], P('table', 'dp')
The draws below stay inside these ranges and needn't reach their ends.
Inputs may be any that keep to these rules, and one draw needn't show every extreme that they name: `served_ids`: the 64 rows that one owner serves one requester are distinct, and exactly 2 of them lie in each of the 32 runs of 128 consecutive rows. `block_fill`: on each device the blocks with positive fill come first; in every table index some device has all 16 slots live and some device has none. Over blocks with positive fill: one device sends at most 1 block to one destination, reached in every draw, and each device receives exactly 8 blocks in all from the devices of its table index.
All inputs are finite; a program needn't handle non-finite values.
Results may differ from the reference program's by a relative error of at most 0.02.
Values may be sent and summed in bfloat16 or wider, within the bound.
A program may use at most 128 MiB of HBM per device.

```python
import jax
import jax.numpy as jnp
from jax import lax

D = 512
H = 4
QK = 64
BLK = 128
BLK_DEV = 16
CAP = 64
ROWS_DEV = 4096
WORK_DEV = 8
ROWS = 32768
N_DP = 32
N_TABLE = 8


def route_plan(key):

    def one_group(group_key):
        label_key, pair_key, length_key, full_key, part_key = jax.random.split(group_key, 5)
        labels = jax.random.permutation(label_key, N_DP).astype(jnp.int32)
        order = jax.random.permutation(pair_key, N_DP).astype(jnp.int32)
        first = jax.random.randint(length_key, (N_DP // 2,), 0, BLK_DEV + 1).astype(jnp.int32)
        first = first.at[0].set(BLK_DEV)
        paired = jnp.stack([first, BLK_DEV - first], axis=1).reshape(N_DP)
        lengths = jnp.zeros((N_DP,), jnp.int32).at[order].set(paired)
        prefix = jnp.cumsum(lengths) - lengths
        slot_rank = jnp.arange(BLK_DEV, dtype=jnp.int32)
        sends = labels[jnp.mod(prefix[:, None] + slot_rank[None, :], N_DP)]
        partial_fill = jax.random.randint(part_key, (N_DP, BLK_DEV), 1, BLK + 1)
        full_block = jax.random.randint(full_key, (N_DP, BLK_DEV), 0, 4) > 0
        fills = jnp.where(full_block, BLK, partial_fill)
        fills = jnp.where(slot_rank[None, :] < lengths[:, None], fills, 0)
        return (sends.astype(jnp.int32), fills.astype(jnp.int32))
    group_keys = jax.vmap(lambda index_value: jax.random.fold_in(key, index_value))(jnp.arange(N_TABLE))
    sends, fills = jax.vmap(one_group)(group_keys)
    return (jnp.transpose(sends, (1, 0, 2)), jnp.transpose(fills, (1, 0, 2)))


def draw_destination(key, part):
    return route_plan(key)[0]


def draw_block_fill(key, part):
    return route_plan(key)[1]


def draw_served_ids(key, part):
    key = jax.random.fold_in(key, 7)
    span = ROWS_DEV // N_DP
    per_run = CAP // N_DP
    count = N_DP * N_TABLE * N_TABLE
    pick_key, order_key = jax.random.split(key)
    pick_keys = jax.random.split(pick_key, count * N_DP)
    offsets = jax.vmap(lambda one_key: jax.random.permutation(one_key, span)[:per_run])(pick_keys).reshape(count, CAP)
    bases = jnp.repeat(jnp.arange(N_DP, dtype=jnp.int32) * span, per_run)
    ids = offsets.astype(jnp.int32) + bases[None, :]
    order_keys = jax.random.split(order_key, count)
    shuffled = jax.vmap(lambda one_key, row: row[jax.random.permutation(one_key, CAP)])(order_keys, ids)
    return shuffled.reshape(N_DP, N_TABLE, N_TABLE, CAP).astype(jnp.int32)


def plant(entries, own_key, smallest, top_value):
    longest = entries.shape.index(max(entries.shape))
    spots = []
    for shift in (0, 1):
        where = [jax.random.randint(jax.random.fold_in(own_key, axis), (), 0, length) for axis, length in enumerate(entries.shape)]
        where[longest] = (where[longest] + shift) % entries.shape[longest]
        spots.append(tuple(where))
    return entries.at[spots[0]].set(smallest).at[spots[1]].set(top_value)


def block_scale(own_key, extent, shards, smallest, largest):
    loudness = 1.0
    for dim, shards_of in shards:
        heights = jax.random.uniform(jax.random.fold_in(jax.random.fold_in(own_key, 6), dim), (shards_of,), jnp.float32, smallest / len(shards), largest / len(shards))
        loudness = loudness * jnp.repeat(jnp.exp(heights), extent[dim] // shards_of).reshape((-1,) + (1,) * (len(extent) - 1 - dim))
    return loudness


def scatter_about(key, dims, scale, reach, shards=(), held_as=jnp.bfloat16):
    drawn = jax.random.normal(key, dims, jnp.float32) * scale
    if len(shards) > 0:
        drawn = block_scale(key, dims, shards, -0.22, 0.18) * drawn
    return jnp.clip(drawn, min=-reach, max=reach).astype(held_as)


def setup_inputs(seed: int = 0) -> dict:
    splits = jax.random.split(jax.random.key(seed), 11)
    return {
        "embedding_table": scatter_about(splits[0], (ROWS, D), 1.0, 6.0, ((0, 8),)),
        "served_ids": draw_served_ids(jax.random.fold_in(splits[10], 71), 0),
        "event_slot": plant(jax.random.randint(splits[2], (N_DP, N_TABLE, BLK_DEV, BLK), 0, N_TABLE * CAP), jax.random.fold_in(splits[2], 1), 0, (N_TABLE * CAP) - 1).astype(jnp.int32),
        "block_fill": draw_block_fill(jax.random.fold_in(splits[10], 71), 0),
        "destination": draw_destination(jax.random.fold_in(splits[10], 71), 0),
        "target": scatter_about(splits[5], (N_DP, N_TABLE, BLK_DEV, BLK, D), 0.25, 1.5, ((0, 32), (1, 8))),
        "w_in": scatter_about(splits[6], (D, 2 * D + 2 * H * QK), D ** -0.5, 0.25),
        "w_out": scatter_about(splits[7], (D, D), D ** -0.5, 0.25),
        "gain_in": jnp.clip(1.0 + 0.18 * jax.random.normal(splits[8], (D,), jnp.float32), 0.1, 1.9),
        "gain_out": jnp.clip(1.0 + 0.18 * jax.random.normal(splits[9], (D,), jnp.float32), 0.1, 1.9),
    }


epsilon = 1e-05

def layer_norm(values, gain_vector):
    centre = lax.optimization_barrier(jnp.mean(values, axis=-1, keepdims=True))
    shifted = values - centre
    spread = lax.optimization_barrier(jnp.mean(shifted * shifted, axis=-1, keepdims=True))
    return shifted * lax.rsqrt(spread + epsilon) * gain_vector

def block_layer(inputs, fill_counts, w_in, w_out, gain_in, gain_out):
    block_count, block_len, feature_dim = inputs.shape
    query_width = H * QK
    values = inputs.astype(jnp.float32)
    normed = layer_norm(values, gain_in).astype(jnp.bfloat16)
    projected = jax.nn.silu(jnp.einsum('bed,df->bef', normed.astype(jnp.float32), w_in.astype(jnp.float32)))
    gate_part = projected[..., :feature_dim]
    value_part = projected[..., feature_dim:2 * feature_dim].astype(jnp.bfloat16).reshape(block_count, block_len, H, feature_dim // H)
    query_part = projected[..., 2 * feature_dim:2 * feature_dim + query_width].astype(jnp.bfloat16).reshape(block_count, block_len, H, QK)
    key_part = projected[..., 2 * feature_dim + query_width:].astype(jnp.bfloat16).reshape(block_count, block_len, H, QK)
    scores = jnp.einsum('bqhc,bkhc->bhqk', query_part.astype(jnp.float32), key_part.astype(jnp.float32)) * QK ** (-0.5)
    position = jnp.arange(block_len)
    allowed = (position[:, None] >= position[None, :])[None, :, :] & (position[None, None, :] < fill_counts[:, None, None])
    attention = jnp.where(allowed[:, None, :, :], jax.nn.silu(scores) / block_len, 0.0).astype(jnp.bfloat16)
    attended = jnp.einsum('bhqk,bkhc->bqhc', attention.astype(jnp.float32), value_part.astype(jnp.float32)).reshape(block_count, block_len, feature_dim)
    gated_rows = (layer_norm(attended, gain_out) * gate_part).astype(jnp.bfloat16)
    return values + jnp.einsum('bed,df->bef', gated_rows.astype(jnp.float32), w_out.astype(jnp.float32))

def block_grads(inputs, fill_counts, aims, w_in, w_out, gain_in, gain_out):
    block_len = inputs.shape[1]
    position = jnp.arange(block_len)
    live_mask = (position[None, :] < fill_counts[:, None]).astype(jnp.float32)

    def loss_of(values_in):
        outputs = block_layer(values_in, fill_counts, w_in, w_out, gain_in, gain_out)
        return (jnp.sum(outputs * aims.astype(jnp.float32) * live_mask[:, :, None]), outputs)
    loss_value, pullback, outputs = jax.vjp(loss_of, inputs, has_aux=True)
    input_grads = pullback(jnp.ones_like(loss_value))[0]
    chosen = (position[None, :] == fill_counts[:, None] - 1).astype(jnp.float32)
    summary = lax.optimization_barrier(jnp.sum(outputs * chosen[:, :, None], axis=1)).astype(jnp.bfloat16)
    return (summary, input_grads)

def reference(embedding_table, served_ids, event_slot, block_fill, destination, target, w_in, w_out, gain_in, gain_out):
    feature_dim = embedding_table.shape[1]
    owner_base = (jnp.arange(N_TABLE) * ROWS_DEV).astype(jnp.int32)
    requests = jnp.transpose(served_ids, (0, 2, 1, 3)).reshape(N_DP * N_TABLE, N_TABLE, CAP)
    slot_all = event_slot.reshape(N_DP * N_TABLE, BLK_DEV, BLK)
    fill_all = block_fill.reshape(N_DP * N_TABLE, BLK_DEV)
    aim_all = target.reshape(N_DP * N_TABLE, BLK_DEV, BLK, feature_dim)

    def one_device(pieces):
        requested, slot_index, fill_counts, aims = pieces
        unique_rows = jnp.take(embedding_table, (requested + owner_base[:, None]).reshape(-1), axis=0)
        inputs = jnp.take(unique_rows, slot_index.reshape(-1), axis=0).reshape(BLK_DEV, BLK, feature_dim)
        summary, input_grads = block_grads(inputs, fill_counts, aims, w_in, w_out, gain_in, gain_out)
        unique_grads = jax.ops.segment_sum(input_grads.astype(jnp.float32).reshape(-1, feature_dim), slot_index.reshape(-1), num_segments=N_TABLE * CAP).astype(jnp.bfloat16)
        return (summary, unique_grads)
    summaries, unique_grads = lax.map(one_device, (requests, slot_all, fill_all, aim_all))
    summaries = summaries.reshape(N_DP, N_TABLE, BLK_DEV, feature_dim)
    unique_grads = unique_grads.reshape(N_DP, N_TABLE, N_TABLE, CAP, feature_dim)

    def add_owner_terms(total, pieces):
        requested_rows, returned = pieces
        flat_rows = (requested_rows + owner_base[:, None, None]).reshape(-1)
        flat_grads = jnp.transpose(returned, (1, 0, 2, 3)).reshape(-1, feature_dim).astype(jnp.float32)
        return (total + jax.ops.segment_sum(flat_grads, flat_rows, num_segments=N_TABLE * ROWS_DEV), None)
    row_total, ignored = lax.scan(add_owner_terms, jnp.zeros((N_TABLE * ROWS_DEV, feature_dim), jnp.float32), (served_ids, unique_grads))

    def place_group(summary_group, fill_group, destination_group):
        live_flat = fill_group.reshape(-1) > 0
        target_flat = destination_group.reshape(-1)
        onehot = ((target_flat[:, None] == jnp.arange(N_DP)[None, :]) & live_flat[:, None]).astype(jnp.int32)
        earlier = jnp.cumsum(onehot, axis=0) - onehot
        position = lax.optimization_barrier(jnp.sum(earlier * onehot, axis=1))
        device_index = jnp.where(live_flat, target_flat, N_DP)
        placed = jnp.zeros((N_DP, WORK_DEV, feature_dim), jnp.bfloat16)
        return placed.at[device_index, position].set(summary_group.reshape(-1, feature_dim), mode='drop')
    placed_all = jax.vmap(place_group, in_axes=(1, 1, 1), out_axes=1)(summaries, block_fill, destination)
    return (placed_all, row_total.reshape(N_TABLE, ROWS_DEV, feature_dim))
```

```python
import functools

import jax
import jax.numpy as jnp
from jax import lax
from jax.experimental import pallas as pl
from jax.experimental.pallas import tpu as pltpu
from jax.sharding import PartitionSpec as P

H = 4
QK = 64
PACK = 16
LANES = 128
EPS = 1e-05
F32 = jnp.float32
BF16 = jnp.bfloat16
VMEM_BYTES = 48 * 1024 * 1024


def dot(a, b, ca=1, cb=0):
    return lax.dot_general(a, b, (((ca,), (cb,)), ((), ())), preferred_element_type=F32)


def iota(shape, axis):
    return lax.broadcasted_iota(jnp.int32, shape, axis)


def onehot(condition):
    return jnp.where(condition, 1.0, 0.0).astype(BF16)


def sigmoid(x):
    return 0.5 * jnp.tanh(0.5 * x) + 0.5


def column_of(row):
    n = row.shape[1]
    here = iota((n, n), 0) == iota((n, n), 1)
    return jnp.sum(jnp.where(here, row, 0.0), axis=1, keepdims=True)


def fill_order(ids_ref, order_ref, local_ref, run):
    table_count, cap = ids_ref.shape
    unique = table_count * cap
    for t in range(table_count):
        row = ids_ref[t : t + 1, :].astype(F32)
        column = column_of(row)
        rank = jnp.sum(jnp.where(row < column, 1.0, 0.0), axis=1, keepdims=True).astype(jnp.int32)
        place = (rank // 2) * (2 * table_count) + 2 * t + rank % 2
        order_ref[t * cap : (t + 1) * cap, :] = onehot(iota((cap, unique), 1) == place)
        if local_ref is not None:
            local = column.astype(jnp.int32) % run
            local_ref[t * cap : (t + 1) * cap, :] = jnp.broadcast_to(
                local.astype(F32), (cap, run)
            ).astype(BF16)


def greet(dp_count, table_count):
    barrier = pltpu.get_barrier_semaphore()
    me_d, me_t = lax.axis_index("dp"), lax.axis_index("table")

    def signal_dp(step, carry):
        pl.semaphore_signal(barrier, inc=1, device_id={"dp": (me_d + step) % dp_count})
        return carry

    lax.fori_loop(1, dp_count, signal_dp, 0)
    for step in range(1, table_count):
        pl.semaphore_signal(barrier, inc=1, device_id={"table": (me_t + step) % table_count})
    pl.semaphore_wait(barrier, dp_count + table_count - 2)


class Exchange:
    def __init__(self, axis, count, source, target, block, send, recv):
        self.axis, self.count, self.block = axis, count, block
        self.source, self.target, self.send, self.recv = source, target, send, recv
        self.me = lax.axis_index(axis)

    def rows(self, index):
        return pl.ds(pl.multiple_of(index * self.block, self.block), self.block)

    def copy(self, peer, slot):
        return pltpu.make_async_remote_copy(
            src_ref=self.source.at[self.rows(peer)],
            dst_ref=self.target.at[self.rows(slot)],
            send_sem=self.send.at[peer],
            recv_sem=self.recv.at[slot],
            device_id={self.axis: peer},
        )

    def loop(self, step_fn):
        def step(index, carry):
            step_fn((self.me + index) % self.count)
            return carry

        lax.fori_loop(1, self.count, step, 0)

    def start(self):
        self.loop(lambda peer: self.copy(peer, self.me).start())
        self.target[self.rows(self.me), :] = self.source[self.rows(self.me), :]

    def wait_recv(self):
        self.loop(lambda peer: self.copy(peer, peer).wait_recv())

    def wait_send(self):
        self.loop(lambda peer: self.copy(peer, self.me).wait_send())


def fetch_kernel(
    dp_count, ids_ref, table_ref, rows_ref, picks_ref,
    table_v, order, local, picks, sorted_rows, served,
    load_sem, send_t, recv_t, send_d, recv_d,
):
    table_count, cap = ids_ref.shape
    shard_rows, width = table_ref.shape
    unique = table_count * cap
    run = shard_rows // dp_count
    group = min(8, dp_count)
    span, part = group * run, group * 2 * table_count
    loads = []
    for g in range(dp_count // group):
        load = pltpu.make_async_copy(
            table_ref.at[pl.ds(g * span, span)], table_v.at[pl.ds(g * span, span)], load_sem.at[g]
        )
        load.start()
        loads.append(load)
    fill_order(ids_ref, order, local, run)
    index = dot(order[...], local[...], 0, 0)
    picks[...] = onehot(index.astype(jnp.int32) == iota((unique, run), 1))
    greet(dp_count, table_count)
    pick_exchange = Exchange("dp", dp_count, picks, picks_ref, 2 * table_count, send_d, recv_d)
    pick_exchange.start()
    for g, load in enumerate(loads):
        mine = picks[g * part : (g + 1) * part, :]
        wide = jnp.concatenate([mine] * group, axis=1)
        same = iota((part, span), 0) // (2 * table_count) == iota((part, span), 1) // run
        load.wait()
        sorted_rows[g * part : (g + 1) * part, :] = dot(
            jnp.where(same, wide, jnp.zeros_like(wide)), table_v[g * span : (g + 1) * span, :]
        ).astype(BF16)
    served[...] = dot(order[...], sorted_rows[...]).astype(BF16)
    row_exchange = Exchange("table", table_count, served, rows_ref, cap, send_t, recv_t)
    row_exchange.start()
    row_exchange.wait_recv()
    pick_exchange.wait_recv()
    row_exchange.wait_send()
    pick_exchange.wait_send()


def compute_kernel(
    fill_ref, rows_ref, slot_ref, fills_ref, dest_ref, aims_ref, w_in_ref, w_out_ref,
    gain_in_ref, gain_out_ref, grads_ref, message_ref,
    proj, slope, hat, inv, tall, spread, dproj, last,
):
    unique, width = rows_ref.shape
    block_count, length = slot_ref.shape
    query = H * QK
    cols = 2 * width + 2 * query
    head = width // H
    gain_in = gain_in_ref[...]
    gain_out = gain_out_ref[...]

    chunk = min(128, unique)

    def project(i, carry):
        rows = pl.ds(pl.multiple_of(i * chunk, chunk), chunk)
        x = rows_ref[rows, :].astype(F32)
        shifted = x - jnp.mean(x, axis=1, keepdims=True)
        scale = lax.rsqrt(jnp.mean(shifted * shifted, axis=1, keepdims=True) + EPS)
        normal = shifted * scale
        hat[rows, :] = normal
        inv[rows, :] = jnp.broadcast_to(scale, (chunk, LANES))
        normed = (normal * gain_in).astype(BF16)
        for c in range(0, cols, width):
            pre = dot(normed, w_in_ref[:, c : c + width])
            sig = sigmoid(pre)
            act = pre * sig
            proj[rows, c : c + width] = act.astype(BF16)
            slope[rows, c : c + width] = sig + act * (1.0 - sig)
        return carry

    lax.fori_loop(0, unique // chunk, project, 0)

    causal = iota((length, length), 0) >= iota((length, length), 1)
    key_lane = iota((length, length), 1)
    query_head = iota((length, query), 1) // QK
    position = iota((length, 1), 0)
    slots = slot_ref[...].astype(F32)
    eye = iota((length, length), 0) == iota((length, length), 1)

    def one_block(b):
        rows = pl.ds(pl.multiple_of(b * length, length), length)
        fill = fill_ref[b]
        slot_row = slot_ref[pl.ds(b, 1), :].astype(F32)
        slot_col = jnp.sum(jnp.where(eye, slot_row, 0.0), axis=1, keepdims=True).astype(jnp.int32)
        here = onehot(iota((length, unique), 1) == slot_col)
        aim = aims_ref[rows, :]
        live_aim = jnp.where(position < fill, aim, jnp.zeros_like(aim))
        spread[rows, cols:] = live_aim
        dgated = dot(live_aim, w_out_ref[...], 1, 1)
        gate = dot(here, proj[:, :width])
        value = dot(here, proj[:, width : 2 * width]).astype(BF16)
        qk = dot(here, proj[:, 2 * width :]).astype(BF16)
        q, k = qk[:, :query], qk[:, query:]
        zero = jnp.zeros_like(q)
        q4 = jnp.concatenate([jnp.where(query_head == h, q, zero) for h in range(H)], axis=0)
        k4 = jnp.concatenate([jnp.where(query_head == h, k, zero) for h in range(H)], axis=0)
        raw = dot(q4, k, 1, 1)
        seen = causal & (key_lane < fill)
        weights, slopes, attended = [], [], []
        for h in range(H):
            s = raw[h * length : (h + 1) * length, :] * QK ** (-0.5)
            sig = sigmoid(s)
            act = s * sig
            weight = jnp.where(seen, act * (1.0 / length), 0.0).astype(BF16)
            weights.append(weight)
            slopes.append(
                jnp.where(seen, (sig + act * (1.0 - sig)) * (QK ** (-0.5) / length), 0.0)
            )
            attended.append(dot(weight, value[:, h * head : (h + 1) * head]))
        attended = jnp.concatenate(attended, axis=1)
        shifted = attended - jnp.mean(attended, axis=1, keepdims=True)
        scale = lax.rsqrt(jnp.mean(shifted * shifted, axis=1, keepdims=True) + EPS)
        normal = shifted * scale
        out = normal * gain_out
        last[pl.ds(b, 1), :] = jnp.sum(
            jnp.where(position == fill - 1, out * gate, 0.0), axis=0, keepdims=True
        )
        spread[rows, :width] = (dgated * out).astype(BF16)
        dnormal = dgated * gate * gain_out
        dattended = scale * (
            dnormal
            - jnp.mean(dnormal, axis=1, keepdims=True)
            - normal * jnp.mean(dnormal * normal, axis=1, keepdims=True)
        )
        dattended = dattended.astype(BF16)
        dscores = []
        for h in range(H):
            part = slice(h * head, (h + 1) * head)
            dweight = dot(dattended[:, part], value[:, part], 1, 1)
            dscores.append((dweight * slopes[h]).astype(BF16))
            spread[rows, width + h * head : width + (h + 1) * head] = dot(
                weights[h], dattended[:, part], 0, 0
            ).astype(BF16)
        spread[rows, 2 * width : 2 * width + query] = dot(
            jnp.concatenate(dscores, axis=1), k4
        ).astype(BF16)
        spread[rows, 2 * width + query : cols] = dot(
            jnp.concatenate(dscores, axis=0), q4, 0, 0
        ).astype(BF16)

    def pair(i, carry):
        one_block(2 * i)
        one_block(2 * i + 1)
        return carry

    lax.fori_loop(0, block_count // 2, pair, 0)

    tile = min(256, unique)
    for r in range(0, unique, tile):
        rows = slice(r, r + tile)
        for b in range(block_count):
            tall[:, b * length : (b + 1) * length] = onehot(
                iota((tile, length), 0) + r == slot_ref[b : b + 1, :]
            )
        for c in range(0, cols, width):
            total = dot(tall[...], spread[:, c : c + width])
            dproj[:, c : c + width] = (total * slope[rows, c : c + width]).astype(BF16)
        dhat = dot(dproj[...], w_in_ref[...], 1, 1) * gain_in
        normal = hat[rows, :]
        scale = inv[rows, :1]
        dx = scale * (
            dhat
            - jnp.mean(dhat, axis=1, keepdims=True)
            - normal * jnp.mean(dhat * normal, axis=1, keepdims=True)
        )
        grads_ref[rows, :] = (dx + dot(tall[...], spread[:, cols:])).astype(BF16)

    fills = fills_ref[...]
    fill_col = column_of(fills.astype(F32)).astype(jnp.int32)
    last_slot = jnp.sum(
        jnp.where(iota((block_count, length), 1) == fill_col - 1, slots, 0.0),
        axis=1,
        keepdims=True,
    ).astype(jnp.int32)
    last_rows = dot(onehot(iota((block_count, unique), 1) == last_slot), rows_ref[...])
    summary = (last_rows + dot(last[...].astype(BF16), w_out_ref[...])).astype(BF16)
    total_rows = message_ref.shape[0]
    row = iota((total_rows, block_count), 0)
    chosen = (row // PACK == dest_ref[...]) & (fills > 0)
    flag = jnp.sum(jnp.where(chosen & (row % PACK == width // LANES), 1.0, 0.0), axis=1, keepdims=True)
    message = jnp.broadcast_to(flag, message_ref.shape)
    for i in range(width // LANES):
        message = message + dot(
            onehot(chosen & (row % PACK == i)), summary[:, i * LANES : (i + 1) * LANES]
        )
    message_ref[...] = message.astype(BF16)


def return_kernel(
    dp_count, ids_ref, grads_ref, message_ref, picks_ref, summary_ref, total_ref,
    order, home, ordered, arrived, letters,
    send_t, recv_t, send_d, recv_d, send_m, recv_m,
):
    table_count, cap = ids_ref.shape
    unique, width = grads_ref.shape
    greet(dp_count, table_count)
    home_exchange = Exchange("table", table_count, grads_ref, home, cap, send_t, recv_t)
    home_exchange.start()
    letter_exchange = Exchange("dp", dp_count, message_ref, letters, PACK, send_m, recv_m)
    letter_exchange.start()
    fill_order(ids_ref, order, None, picks_ref.shape[1])
    home_exchange.wait_recv()
    ordered[...] = dot(order[...], home[...], 0, 0).astype(BF16)
    total_exchange = Exchange("dp", dp_count, ordered, arrived, 2 * table_count, send_d, recv_d)
    total_exchange.start()
    letter_exchange.wait_recv()
    rows = letters.shape[0]
    row, col = iota((rows, rows), 0), iota((rows, rows), 1)
    flag_col = col % PACK == width // LANES
    rank = dot(onehot(flag_col & (col // PACK < row // PACK)), letters[...])
    present = dot(onehot(flag_col & (col // PACK == row // PACK)), letters[...])
    lane = iota((rows, LANES), 1)
    wanted = (present > 0.5) & (rank.astype(jnp.int32) == lane)
    kind = iota((rows, LANES), 0) % PACK
    work = summary_ref.shape[0]
    for i in range(width // LANES):
        part = dot(onehot(wanted & (kind == i)), letters[...], 0, 0)
        summary_ref[:, i * LANES : (i + 1) * LANES] = part[:work, :].astype(BF16)
    total_exchange.wait_recv()
    total_ref[...] = dot(picks_ref[...], arrived[...], 0, 0)
    home_exchange.wait_send()
    letter_exchange.wait_send()
    total_exchange.wait_send()


def whole(space=pltpu.VMEM):
    return pl.BlockSpec(memory_space=space)


def body(
    embedding_table, served_ids, event_slot, block_fill, destination, target, w_in, w_out,
    gain_in, gain_out,
):
    dp_count, table_count = lax.axis_size("dp"), lax.axis_size("table")
    shard_rows, width = embedding_table.shape
    ids = served_ids[0, 0]
    cap = ids.shape[1]
    unique = table_count * cap
    run = shard_rows // dp_count
    slots = event_slot[0, 0]
    block_count, length = slots.shape
    work_count = block_count // 2
    events = block_count * length
    cols = w_in.shape[1]
    dma = pltpu.SemaphoreType.DMA
    params = functools.partial(pltpu.CompilerParams, vmem_limit_bytes=VMEM_BYTES)
    rows, picks = pl.pallas_call(
        functools.partial(fetch_kernel, dp_count),
        out_shape=(
            jax.ShapeDtypeStruct((unique, width), BF16),
            jax.ShapeDtypeStruct((unique, run), BF16),
        ),
        in_specs=[whole(), whole(pl.ANY)],
        out_specs=(whole(), whole()),
        scratch_shapes=[
            pltpu.VMEM((shard_rows, width), BF16),
            pltpu.VMEM((unique, unique), BF16),
            pltpu.VMEM((unique, run), BF16),
            pltpu.VMEM((unique, run), BF16),
            pltpu.VMEM((unique, width), BF16),
            pltpu.VMEM((unique, width), BF16),
            dma((max(1, dp_count // 8),)),
            dma((table_count,)), dma((table_count,)), dma((dp_count,)), dma((dp_count,)),
        ],
        compiler_params=params(collective_id=0, has_side_effects=True),
        name="fetch",
    )(ids, embedding_table)
    fills = block_fill[0, 0]
    grads, message = pl.pallas_call(
        compute_kernel,
        out_shape=(
            jax.ShapeDtypeStruct((unique, width), BF16),
            jax.ShapeDtypeStruct((dp_count * PACK, LANES), BF16),
        ),
        in_specs=[whole(pltpu.SMEM)] + [whole()] * 9,
        out_specs=(whole(), whole()),
        scratch_shapes=[
            pltpu.VMEM((unique, cols), BF16),
            pltpu.VMEM((unique, cols), F32),
            pltpu.VMEM((unique, width), F32),
            pltpu.VMEM((unique, LANES), F32),
            pltpu.VMEM((min(256, unique), events), BF16),
            pltpu.VMEM((events, cols + width), BF16),
            pltpu.VMEM((min(256, unique), cols), BF16),
            pltpu.VMEM((block_count, width), F32),
        ],
        compiler_params=params(),
        name="compute",
    )(
        fills, rows, slots, fills.reshape(1, -1), destination[0, 0].reshape(1, -1),
        target.reshape(events, width), w_in, w_out, gain_in.reshape(1, -1), gain_out.reshape(1, -1),
    )
    summary, total = pl.pallas_call(
        functools.partial(return_kernel, dp_count),
        out_shape=(
            jax.ShapeDtypeStruct((work_count, width), BF16),
            jax.ShapeDtypeStruct((run, width), F32),
        ),
        in_specs=[whole()] * 4,
        out_specs=(whole(), whole()),
        scratch_shapes=[
            pltpu.VMEM((unique, unique), BF16),
            pltpu.VMEM((unique, width), BF16),
            pltpu.VMEM((unique, width), BF16),
            pltpu.VMEM((unique, width), BF16),
            pltpu.VMEM((dp_count * PACK, LANES), BF16),
            dma((table_count,)), dma((table_count,)), dma((dp_count,)), dma((dp_count,)),
            dma((dp_count,)), dma((dp_count,)),
        ],
        compiler_params=params(collective_id=1, has_side_effects=True),
        name="return_home",
    )(ids, grads, message, picks)
    return (summary.reshape(1, 1, work_count, width), total.reshape(1, run, width))


def solution(mesh):
    return jax.shard_map(
        body,
        mesh=mesh,
        in_specs=(
            P("table", None),
            P("dp", "table", None, None),
            P("dp", "table", None, None),
            P("dp", "table", None),
            P("dp", "table", None),
            P("dp", "table", None, None, None),
            P(), P(), P(), P(),
        ),
        out_specs=(P("dp", "table", None, None), P("table", "dp", None)),
        check_vma=False,
    )
```

```python
import functools

import jax
import jax.numpy as jnp
from jax import lax
from jax.experimental import pallas as pl
from jax.experimental.pallas import tpu as pltpu
from jax.sharding import PartitionSpec as P

H = 4
QK = 64
PACK = 16
LANES = 128
EPS = 1e-05
F32 = jnp.float32
BF16 = jnp.bfloat16
VMEM_BYTES = 48 * 1024 * 1024
PROJECT_ROWS = 128
GATHER_ROWS = 256
BLOCK_GROUP = 2
FINISH_ROWS = 256
PARTS = 2


def dot(a, b, ca=1, cb=0):
    return lax.dot_general(a, b, (((ca,), (cb,)), ((), ())), preferred_element_type=F32)


def iota(shape, axis):
    return lax.broadcasted_iota(jnp.int32, shape, axis)


def onehot(condition):
    return jnp.where(condition, 1.0, 0.0).astype(BF16)


def sigmoid(x):
    return 0.5 * jnp.tanh(0.5 * x) + 0.5


def column_of(row):
    n = row.shape[1]
    here = iota((n, n), 0) == iota((n, n), 1)
    return jnp.sum(jnp.where(here, row, 0.0), axis=1, keepdims=True)


def fill_order(ids_ref, order_ref, local_ref, run):
    table_count, cap = ids_ref.shape
    unique = table_count * cap
    for t in range(table_count):
        row = ids_ref[t : t + 1, :].astype(F32)
        column = column_of(row)
        rank = jnp.sum(jnp.where(row < column, 1.0, 0.0), axis=1, keepdims=True).astype(jnp.int32)
        place = (rank // 2) * (2 * table_count) + 2 * t + rank % 2
        order_ref[t * cap : (t + 1) * cap, :] = onehot(iota((cap, unique), 1) == place)
        if local_ref is not None:
            local = column.astype(jnp.int32) % run
            local_ref[t * cap : (t + 1) * cap, :] = jnp.broadcast_to(
                local.astype(F32), (cap, run)
            ).astype(BF16)


def greet(barrier, dp_count, table_count):
    me_d, me_t = lax.axis_index("dp"), lax.axis_index("table")

    def signal_dp(step, carry):
        pl.semaphore_signal(barrier, inc=1, device_id={"dp": (me_d + step) % dp_count})
        return carry

    lax.fori_loop(1, dp_count, signal_dp, 0)
    for step in range(1, table_count):
        pl.semaphore_signal(barrier, inc=1, device_id={"table": (me_t + step) % table_count})


class Exchange:
    def __init__(self, axis, count, source, target, block, sems):
        self.axis, self.count, self.block = axis, count, block
        self.source, self.target = source, target
        self.send, self.recv = sems
        self.me = lax.axis_index(axis)

    def rows(self, index):
        return pl.ds(pl.multiple_of(index * self.block, self.block), self.block)

    def copy(self, peer, slot):
        return pltpu.make_async_remote_copy(
            src_ref=self.source.at[self.rows(peer)],
            dst_ref=self.target.at[self.rows(slot)],
            send_sem=self.send.at[peer],
            recv_sem=self.recv.at[slot],
            device_id={self.axis: peer},
        )

    def loop(self, step_fn):
        def step(index, carry):
            step_fn((self.me + index) % self.count)
            return carry

        lax.fori_loop(1, self.count, step, 0)

    def start(self):
        self.loop(lambda peer: self.copy(peer, self.me).start())
        self.target[self.rows(self.me), :] = self.source[self.rows(self.me), :]

    def wait_recv(self):
        self.loop(lambda peer: self.copy(peer, peer).wait_recv())

    def wait_send(self):
        self.loop(lambda peer: self.copy(peer, self.me).wait_send())


def prepare(fill_ref, slot_ref, w_out_ref, here, tall, spread, dgated):
    block_count, length = slot_ref.shape
    unique = here.shape[1]
    cols = spread.shape[1] - w_out_ref.shape[0]
    eye = iota((length, length), 0) == iota((length, length), 1)
    position = iota((length, 1), 0)

    def one(b, carry):
        rows = pl.ds(pl.multiple_of(b * length, length), length)
        slot_row = slot_ref[pl.ds(b, 1), :]
        slot_col = jnp.sum(
            jnp.where(eye, slot_row.astype(F32), 0.0), axis=1, keepdims=True
        ).astype(jnp.int32)
        here[rows, :] = onehot(iota((length, unique), 1) == slot_col)
        tall[:, rows] = onehot(iota((unique, length), 0) == slot_row)
        aim = spread[rows, cols:]
        live_aim = jnp.where(position < fill_ref[b], aim, jnp.zeros_like(aim))
        spread[rows, cols:] = live_aim
        dgated[rows, :] = dot(live_aim, w_out_ref[...], 1, 1).astype(BF16)
        return carry

    lax.fori_loop(0, block_count, one, 0)


def project(rows_ref, w_in_ref, gain_in_ref, gain_out_ref, length, proj, slope, hat, inv):
    unique, width = rows_ref.shape
    query = H * QK
    gain_in = gain_in_ref[...]
    half = 0.5 * QK ** (-0.5)
    lane = iota((1, 2 * query), 1)
    factors = [gain_out_ref[...], 1.0 / length, jnp.where(lane < query, half, 1.0)]
    chunk = min(PROJECT_ROWS, unique)

    def step(i, carry):
        rows = pl.ds(pl.multiple_of(i * chunk, chunk), chunk)
        x = rows_ref[rows, :].astype(F32)
        shifted = x - jnp.mean(x, axis=1, keepdims=True)
        scale = lax.rsqrt(jnp.mean(shifted * shifted, axis=1, keepdims=True) + EPS)
        normal = shifted * scale
        hat[rows, :] = normal
        inv[rows, :] = jnp.broadcast_to(scale, (chunk, LANES))
        normed = (normal * gain_in).astype(BF16)
        for c, factor in enumerate(factors):
            part = slice(c * width, (c + 1) * width)
            pre = dot(normed, w_in_ref[:, part])
            sig = sigmoid(pre)
            act = pre * sig
            proj[rows, part] = (act * factor).astype(BF16)
            slope[rows, part] = (sig + act * (1.0 - sig)) * factor
        return carry

    lax.fori_loop(0, unique // chunk, step, 0)


def gather(here, proj, spread):
    events = here.shape[0]
    cols = proj.shape[1]
    chunk = min(GATHER_ROWS, events)
    width = cols // 3

    def step(i, carry):
        rows = pl.ds(pl.multiple_of(i * chunk, chunk), chunk)
        for c in range(0, cols, width):
            spread[rows, c : c + width] = dot(here[rows, :], proj[:, c : c + width]).astype(BF16)
        return carry

    lax.fori_loop(0, events // chunk, step, 0)


def attend(fill_ref, length, spread, dgated, normals, last):
    events, width = dgated.shape
    query = H * QK
    cols = 2 * width + 2 * query
    head = width // H
    block_count = events // length
    group = min(BLOCK_GROUP, block_count)
    causal = iota((length, length), 0) >= iota((length, length), 1)
    key_lane = iota((length, length), 1)
    low = iota((length, LANES), 1) < QK

    def heads(x):
        zero = jnp.zeros((length, LANES), BF16)
        parts = []
        for h in range(H):
            side = h // 2
            mine = x[:, side * LANES : (side + 1) * LANES]
            mine = jnp.where(low if h % 2 == 0 else ~low, mine, zero)
            parts.append(jnp.concatenate([mine, zero] if side == 0 else [zero, mine], axis=1))
        return jnp.concatenate(parts, axis=0)

    def step(i, carry):
        blocks = [group * i + n for n in range(group)]
        rows = [pl.ds(pl.multiple_of(b * length, length), length) for b in blocks]
        fills = [fill_ref[b] for b in blocks]
        n_all = range(group)
        q4, k4, half = [], [], []
        for n in n_all:
            q = spread[rows[n], 2 * width : 2 * width + query]
            k = spread[rows[n], 2 * width + query : cols]
            q4.append(heads(q))
            k4.append(heads(k))
            half.append(dot(q4[n], k, 1, 1))
        weights, slopes, attended = [], [], []
        for n in n_all:
            seen = causal & (key_lane < fills[n])
            ws, ss, parts = [], [], []
            for h in range(H):
                s = half[n][h * length : (h + 1) * length, :]
                up = jnp.where(seen, jnp.tanh(s) + 1.0, 0.0)
                act = s * up
                ws.append(act.astype(BF16))
                ss.append(up * ((s - act) + (s + 1.0)))
                value = spread[rows[n], width + h * head : width + (h + 1) * head]
                parts.append(dot(ws[h], value))
            weights.append(ws)
            slopes.append(ss)
            attended.append(jnp.concatenate(parts, axis=1))
        shifted = [a - jnp.mean(a, axis=1, keepdims=True) for a in attended]
        scale = [lax.rsqrt(jnp.mean(a * a, axis=1, keepdims=True) + EPS) for a in shifted]
        dattended = []
        for n in n_all:
            normal = shifted[n] * scale[n]
            normals[n * length : (n + 1) * length, :] = normal
            gate = spread[rows[n], :width].astype(F32)
            upper = dgated[rows[n], :].astype(F32)
            dnormal = upper * gate
            spread[rows[n], :width] = (upper * normal).astype(BF16)
            where = jnp.maximum(fills[n] - 1, 0)
            last[pl.ds(blocks[n], 1), :] = normals[pl.ds(n * length + where, 1), :]
            mean = jnp.mean(dnormal, axis=1, keepdims=True)
            along = jnp.mean(dnormal * normal, axis=1, keepdims=True)
            dattended.append((scale[n] * (dnormal - mean - normal * along)).astype(BF16))
        dscores = []
        for n in n_all:
            ds = []
            for h in range(H):
                part = slice(h * head, (h + 1) * head)
                there = slice(width + h * head, width + (h + 1) * head)
                dweight = dot(dattended[n][:, part], spread[rows[n], there], 1, 1)
                ds.append((dweight * slopes[n][h]).astype(BF16))
                spread[rows[n], there] = dot(weights[n][h], dattended[n][:, part], 0, 0).astype(BF16)
            dscores.append(ds)
        for n in n_all:
            spread[rows[n], 2 * width : 2 * width + query] = dot(
                jnp.concatenate(dscores[n], axis=1), k4[n]
            ).astype(BF16)
            spread[rows[n], 2 * width + query : cols] = dot(
                jnp.concatenate(dscores[n], axis=0), q4[n], 0, 0
            ).astype(BF16)
        return carry

    lax.fori_loop(0, block_count // group, step, 0)


def write_letters(fills_ref, dest_ref, slot_ref, rows_ref, w_out_ref, proj, last, message):
    block_count, length = slot_ref.shape
    unique, width = rows_ref.shape
    fills = fills_ref[...]
    fill_col = column_of(fills.astype(F32)).astype(jnp.int32)
    last_slot = jnp.sum(
        jnp.where(iota((block_count, length), 1) == fill_col - 1, slot_ref[...].astype(F32), 0.0),
        axis=1,
        keepdims=True,
    ).astype(jnp.int32)
    pick = onehot(iota((block_count, unique), 1) == last_slot)
    gated = (last[...] * dot(pick, proj[:, :width])).astype(BF16)
    summary = (dot(pick, rows_ref[...]) + dot(gated, w_out_ref[...])).astype(BF16)
    row = iota((message.shape[0], block_count), 0)
    chosen = (row // PACK == dest_ref[...]) & (fills > 0)
    flag = jnp.sum(
        jnp.where(chosen & (row % PACK == width // LANES), 1.0, 0.0), axis=1, keepdims=True
    )
    letter = jnp.broadcast_to(flag, message.shape)
    for i in range(width // LANES):
        letter = letter + dot(
            onehot(chosen & (row % PACK == i)), summary[:, i * LANES : (i + 1) * LANES]
        )
    message[...] = letter.astype(BF16)


def read_letters(letters, summary_ref):
    rows = letters.shape[0]
    work, width = summary_ref.shape
    row, col = iota((rows, rows), 0), iota((rows, rows), 1)
    flag_col = col % PACK == width // LANES
    rank = dot(onehot(flag_col & (col // PACK < row // PACK)), letters[...])
    present = dot(onehot(flag_col & (col // PACK == row // PACK)), letters[...])
    wanted = (present > 0.5) & (rank.astype(jnp.int32) == iota((rows, LANES), 1))
    kind = iota((rows, LANES), 0) % PACK
    for i in range(width // LANES):
        part = dot(onehot(wanted & (kind == i)), letters[...], 0, 0)
        summary_ref[:, i * LANES : (i + 1) * LANES] = part[:work, :].astype(BF16)


def finish(w_in_ref, gain_in_ref, tall, spread, slope, hat, inv, dproj, grads):
    unique, width = hat.shape
    cols = slope.shape[1]
    parts, part_width = grads.shape[0], grads.shape[2]
    tile = min(FINISH_ROWS, unique)
    for r in range(0, unique, tile):
        rows = slice(r, r + tile)
        for c in range(0, cols, width):
            total = dot(tall[rows, :], spread[:, c : c + width])
            dproj[:, c : c + width] = (total * slope[rows, c : c + width]).astype(BF16)
        straight = dot(tall[rows, :], spread[:, cols:])
        dhat = dot(dproj[...], w_in_ref[...], 1, 1) * gain_in_ref[...]
        normal = hat[rows, :]
        scale = inv[rows, :1]
        mean = jnp.mean(dhat, axis=1, keepdims=True)
        along = jnp.mean(dhat * normal, axis=1, keepdims=True)
        dx = (scale * (dhat - mean - normal * along) + straight).astype(BF16)
        for p in range(parts):
            grads[p, rows, :] = dx[:, p * part_width : (p + 1) * part_width]


def step_kernel(
    dp_count,
    fill_ref, ids_ref, slot_ref, fills_ref, dest_ref, gain_in_ref, gain_out_ref,
    table_ref, aims_ref, w_in_hbm, w_out_hbm,
    summary_ref, total_ref,
    table_v, w_in_ref, w_out_ref, order, local, picks, picks_in, sorted_rows, served, rows_ref,
    here, tall, spread, dgated, proj, slope, hat, inv, normals, last, dproj,
    message, letters, grads, home, ordered, arrived,
    table_sem, load_sem, row_sems, pick_sems, letter_sems, home_sems, total_sems,
):
    table_count, cap = ids_ref.shape
    shard_rows, width = table_ref.shape
    cols = w_in_ref.shape[1]
    unique = table_count * cap
    run = shard_rows // dp_count
    length = slot_ref.shape[1]
    group = min(8, dp_count)
    span, part = group * run, group * 2 * table_count
    loads = [
        pltpu.make_async_copy(
            table_ref.at[pl.ds(g * span, span)], table_v.at[pl.ds(g * span, span)], table_sem.at[g]
        )
        for g in range(dp_count // group)
    ]
    w_out_load = pltpu.make_async_copy(w_out_hbm, w_out_ref, load_sem.at[0])
    aims_load = pltpu.make_async_copy(
        aims_ref, spread.at[:, pl.ds(cols, width)], load_sem.at[1]
    )
    w_in_load = pltpu.make_async_copy(w_in_hbm, w_in_ref, load_sem.at[2])
    for load in loads + [w_out_load, aims_load, w_in_load]:
        load.start()
    barrier = pltpu.get_barrier_semaphore()
    greet(barrier, dp_count, table_count)

    def pair(sems):
        return sems.at[0], sems.at[1]

    fill_order(ids_ref, order, local, run)
    index = dot(order[...], local[...], 0, 0)
    picks[...] = onehot(index.astype(jnp.int32) == iota((unique, run), 1))
    for g, load in enumerate(loads):
        mine = picks[g * part : (g + 1) * part, :]
        wide = jnp.concatenate([mine] * group, axis=1)
        same = iota((part, span), 0) // (2 * table_count) == iota((part, span), 1) // run
        load.wait()
        sorted_rows[g * part : (g + 1) * part, :] = dot(
            jnp.where(same, wide, jnp.zeros_like(wide)), table_v[g * span : (g + 1) * span, :]
        ).astype(BF16)
    served[...] = dot(order[...], sorted_rows[...]).astype(BF16)
    pl.semaphore_wait(barrier, dp_count + table_count - 2)
    row_exchange = Exchange("table", table_count, served, rows_ref, cap, pair(row_sems))
    row_exchange.start()
    pick_exchange = Exchange("dp", dp_count, picks, picks_in, 2 * table_count, pair(pick_sems))
    pick_exchange.start()

    w_out_load.wait()
    aims_load.wait()
    prepare(fill_ref, slot_ref, w_out_ref, here, tall, spread, dgated)
    w_in_load.wait()
    row_exchange.wait_recv()
    project(rows_ref, w_in_ref, gain_in_ref, gain_out_ref, length, proj, slope, hat, inv)
    gather(here, proj, spread)
    attend(fill_ref, length, spread, dgated, normals, last)
    write_letters(fills_ref, dest_ref, slot_ref, rows_ref, w_out_ref, proj, last, message)
    letter_exchange = Exchange("dp", dp_count, message, letters, PACK, pair(letter_sems))
    letter_exchange.start()
    finish(w_in_ref, gain_in_ref, tall, spread, slope, hat, inv, dproj, grads)

    parts = grads.shape[0]
    part_width = width // parts
    homes, totals = [], []
    for p in range(parts):
        homes.append(
            Exchange("table", table_count, grads.at[p], home.at[p], cap, pair(home_sems.at[p]))
        )
        totals.append(
            Exchange(
                "dp", dp_count, ordered.at[p], arrived.at[p], 2 * table_count, pair(total_sems.at[p])
            )
        )
        homes[p].start()
    for p in range(parts):
        homes[p].wait_recv()
        ordered[p, :, :] = dot(order[...], home[p, :, :], 0, 0).astype(BF16)
        totals[p].start()
    letter_exchange.wait_recv()
    read_letters(letters, summary_ref)
    pick_exchange.wait_recv()
    for p in range(parts):
        totals[p].wait_recv()
        total_ref[:, p * part_width : (p + 1) * part_width] = dot(
            picks_in[...], arrived[p, :, :], 0, 0
        )
    for exchange in [row_exchange, pick_exchange, letter_exchange] + homes + totals:
        exchange.wait_send()


def whole(space=pltpu.VMEM):
    return pl.BlockSpec(memory_space=space)


def body(
    embedding_table, served_ids, event_slot, block_fill, destination, target, w_in, w_out,
    gain_in, gain_out,
):
    dp_count, table_count = lax.axis_size("dp"), lax.axis_size("table")
    shard_rows, width = embedding_table.shape
    ids = served_ids[0, 0]
    cap = ids.shape[1]
    unique = table_count * cap
    run = shard_rows // dp_count
    slots = event_slot[0, 0]
    block_count, length = slots.shape
    work_count = block_count // 2
    events = block_count * length
    cols = w_in.shape[1]
    parts, part_width = PARTS, width // PARTS
    dma = pltpu.SemaphoreType.DMA
    vmem = pltpu.VMEM
    fills = block_fill[0, 0]
    summary, total = pl.pallas_call(
        functools.partial(step_kernel, dp_count),
        out_shape=(
            jax.ShapeDtypeStruct((work_count, width), BF16),
            jax.ShapeDtypeStruct((run, width), F32),
        ),
        in_specs=[whole(pltpu.SMEM)] + [whole()] * 6 + [whole(pl.ANY)] * 4,
        out_specs=(whole(), whole()),
        scratch_shapes=[
            vmem((shard_rows, width), BF16),
            vmem((width, cols), BF16),
            vmem((width, width), BF16),
            vmem((unique, unique), BF16),
            vmem((unique, run), BF16),
            vmem((unique, run), BF16),
            vmem((unique, run), BF16),
            vmem((unique, width), BF16),
            vmem((unique, width), BF16),
            vmem((unique, width), BF16),
        ]
        + compute_scratch(unique, events, cols, width, block_count, length)
        + [
            vmem((dp_count * PACK, LANES), BF16),
            vmem((dp_count * PACK, LANES), BF16),
            vmem((parts, unique, part_width), BF16),
            vmem((parts, unique, part_width), BF16),
            vmem((parts, unique, part_width), BF16),
            vmem((parts, unique, part_width), BF16),
            dma((max(1, dp_count // 8),)),
            dma((3,)),
            dma((2, table_count)),
            dma((2, dp_count)),
            dma((2, dp_count)),
            dma((parts, 2, table_count)),
            dma((parts, 2, dp_count)),
        ],
        compiler_params=pltpu.CompilerParams(
            vmem_limit_bytes=VMEM_BYTES, collective_id=0, has_side_effects=True
        ),
        name="step",
    )(
        fills, ids, slots, fills.reshape(1, -1), destination[0, 0].reshape(1, -1),
        gain_in.reshape(1, -1), gain_out.reshape(1, -1),
        embedding_table, target.reshape(events, width), w_in, w_out,
    )
    return (summary.reshape(1, 1, work_count, width), total.reshape(1, run, width))


def compute_scratch(unique, events, cols, width, block_count, length):
    vmem = pltpu.VMEM
    return [
        vmem((events, unique), BF16),
        vmem((unique, events), BF16),
        vmem((events, cols + width), BF16),
        vmem((events, width), BF16),
        vmem((unique, cols), BF16),
        vmem((unique, cols), F32),
        vmem((unique, width), F32),
        vmem((unique, LANES), F32),
        vmem((BLOCK_GROUP * length, width), F32),
        vmem((block_count, width), F32),
        vmem((min(FINISH_ROWS, unique), cols), BF16),
    ]


def solution(mesh):
    return jax.shard_map(
        body,
        mesh=mesh,
        in_specs=(
            P("table", None),
            P("dp", "table", None, None),
            P("dp", "table", None, None),
            P("dp", "table", None),
            P("dp", "table", None),
            P("dp", "table", None, None, None),
            P(), P(), P(), P(),
        ),
        out_specs=(P("dp", "table", None, None), P("table", "dp", None)),
        check_vma=False,
    )
```

```python
import functools

import jax
import jax.numpy as jnp
from jax import lax
from jax.experimental import pallas as pl
from jax.experimental.pallas import tpu as pltpu
from jax.sharding import PartitionSpec as P

H = 4
QK = 64
PACK = 16
LANES = 128
EPS = 1e-05
F32 = jnp.float32
BF16 = jnp.bfloat16
VMEM_BYTES = 60 * 1024 * 1024
PROJECT_ROWS = 512
GATHER_ROWS = 1024
BLOCK_GROUP = 4
FINISH_ROWS = 256
PARTS = 2


def dot(a, b, ca=1, cb=0):
    return lax.dot_general(a, b, (((ca,), (cb,)), ((), ())), preferred_element_type=F32)


def iota(shape, axis):
    return lax.broadcasted_iota(jnp.int32, shape, axis)


def onehot(condition):
    return jnp.where(condition, 1.0, 0.0).astype(BF16)


def sigmoid(x):
    return 0.5 * jnp.tanh(0.5 * x) + 0.5


def column_of(row):
    n = row.shape[1]
    here = iota((n, n), 0) == iota((n, n), 1)
    return jnp.sum(jnp.where(here, row, 0.0), axis=1, keepdims=True)


def fill_order(ids_ref, order_ref, local_ref, run):
    table_count, cap = ids_ref.shape
    unique = table_count * cap
    for t in range(table_count):
        row = ids_ref[t : t + 1, :].astype(F32)
        column = column_of(row)
        rank = jnp.sum(jnp.where(row < column, 1.0, 0.0), axis=1, keepdims=True).astype(jnp.int32)
        place = (rank // 2) * (2 * table_count) + 2 * t + rank % 2
        order_ref[t * cap : (t + 1) * cap, :] = onehot(iota((cap, unique), 1) == place)
        if local_ref is not None:
            local = column.astype(jnp.int32) % run
            local_ref[t * cap : (t + 1) * cap, :] = jnp.broadcast_to(
                local.astype(F32), (cap, run)
            ).astype(BF16)


def greet(barrier, dp_count, table_count):
    me_d, me_t = lax.axis_index("dp"), lax.axis_index("table")

    def signal_dp(step, carry):
        pl.semaphore_signal(barrier, inc=1, device_id={"dp": (me_d + step) % dp_count})
        return carry

    lax.fori_loop(1, dp_count, signal_dp, 0)
    for step in range(1, table_count):
        pl.semaphore_signal(barrier, inc=1, device_id={"table": (me_t + step) % table_count})


class Exchange:
    def __init__(self, axis, count, source, target, block, sems):
        self.axis, self.count, self.block = axis, count, block
        self.source, self.target = source, target
        self.send, self.recv = sems
        self.me = lax.axis_index(axis)

    def rows(self, index):
        return pl.ds(pl.multiple_of(index * self.block, self.block), self.block)

    def copy(self, peer, slot):
        return pltpu.make_async_remote_copy(
            src_ref=self.source.at[self.rows(peer)],
            dst_ref=self.target.at[self.rows(slot)],
            send_sem=self.send.at[peer],
            recv_sem=self.recv.at[slot],
            device_id={self.axis: peer},
        )

    def loop(self, step_fn):
        def step(index, carry):
            step_fn((self.me + index) % self.count)
            return carry

        lax.fori_loop(1, self.count, step, 0)

    def start(self):
        self.loop(lambda peer: self.copy(peer, self.me).start())
        self.target[self.rows(self.me), :] = self.source[self.rows(self.me), :]

    def wait_recv(self):
        self.loop(lambda peer: self.copy(peer, peer).wait_recv())

    def wait_send(self):
        self.loop(lambda peer: self.copy(peer, self.me).wait_send())


def prepare(slot_ref, here, tall):
    block_count, length = slot_ref.shape
    unique = here.shape[1]
    eye = iota((length, length), 0) == iota((length, length), 1)

    def one(b, carry):
        rows = pl.ds(pl.multiple_of(b * length, length), length)
        slot_row = slot_ref[pl.ds(b, 1), :]
        slot_col = jnp.sum(
            jnp.where(eye, slot_row.astype(F32), 0.0), axis=1, keepdims=True
        ).astype(jnp.int32)
        here[rows, :] = onehot(iota((length, unique), 1) == slot_col)
        tall[:, rows] = onehot(iota((unique, length), 0) == slot_row)
        return carry

    lax.fori_loop(0, block_count, one, 0)


def weigh(fill_ref, length, w_out_ref, spread, dgated):
    events, width = dgated.shape
    cols = spread.shape[1] - width
    position = iota((length, 1), 0)

    def one(b, carry):
        rows = pl.ds(pl.multiple_of(b * length, length), length)
        aim = spread[rows, cols:]
        live_aim = jnp.where(position < fill_ref[b], aim, jnp.zeros_like(aim))
        spread[rows, cols:] = live_aim
        dgated[rows, :] = dot(live_aim, w_out_ref[...], 1, 1).astype(BF16)
        return carry

    lax.fori_loop(0, events // length, one, 0)


def project(rows_ref, w_in_ref, gain_in_ref, gain_out_ref, length, proj, slope, hat, inv):
    unique, width = rows_ref.shape
    query = H * QK
    gain_in = gain_in_ref[...]
    half = 0.5 * QK ** (-0.5)
    lane = iota((1, 2 * query), 1)
    factors = [gain_out_ref[...], 1.0 / length, jnp.where(lane < query, half, 1.0)]
    chunk = min(PROJECT_ROWS, unique)

    def step(i, carry):
        rows = pl.ds(pl.multiple_of(i * chunk, chunk), chunk)
        x = rows_ref[rows, :].astype(F32)
        shifted = x - jnp.mean(x, axis=1, keepdims=True)
        scale = lax.rsqrt(jnp.mean(shifted * shifted, axis=1, keepdims=True) + EPS)
        normal = shifted * scale
        hat[rows, :] = normal
        inv[rows, :] = jnp.broadcast_to(scale, (chunk, LANES))
        normed = (normal * gain_in).astype(BF16)
        for c, factor in enumerate(factors):
            part = slice(c * width, (c + 1) * width)
            pre = dot(normed, w_in_ref[:, part])
            sig = sigmoid(pre)
            act = pre * sig
            proj[rows, part] = (act * factor).astype(BF16)
            slope[rows, part] = (sig + act * (1.0 - sig)) * factor
        return carry

    lax.fori_loop(0, unique // chunk, step, 0)


def gather(here, proj, spread):
    events = here.shape[0]
    cols = proj.shape[1]
    chunk = min(GATHER_ROWS, events)
    width = cols // 3

    def step(i, carry):
        rows = pl.ds(pl.multiple_of(i * chunk, chunk), chunk)
        for c in range(0, cols, width):
            spread[rows, c : c + width] = dot(here[rows, :], proj[:, c : c + width]).astype(BF16)
        return carry

    lax.fori_loop(0, events // chunk, step, 0)


def attend(fill_ref, length, spread, dgated, normals, last):
    events, width = dgated.shape
    query = H * QK
    cols = 2 * width + 2 * query
    head = width // H
    block_count = events // length
    group = min(BLOCK_GROUP, block_count)
    causal = iota((length, length), 0) >= iota((length, length), 1)
    key_lane = iota((length, length), 1)
    low = iota((length, LANES), 1) < QK

    def heads(x):
        zero = jnp.zeros((length, LANES), BF16)
        parts = []
        for h in range(H):
            side = h // 2
            mine = x[:, side * LANES : (side + 1) * LANES]
            mine = jnp.where(low if h % 2 == 0 else ~low, mine, zero)
            parts.append(jnp.concatenate([mine, zero] if side == 0 else [zero, mine], axis=1))
        return jnp.concatenate(parts, axis=0)

    def step(i, carry):
        blocks = [group * i + n for n in range(group)]
        rows = [pl.ds(pl.multiple_of(b * length, length), length) for b in blocks]
        fills = [fill_ref[b] for b in blocks]
        n_all = range(group)
        q4, k4, half = [], [], []
        for n in n_all:
            q = spread[rows[n], 2 * width : 2 * width + query]
            k = spread[rows[n], 2 * width + query : cols]
            q4.append(heads(q))
            k4.append(heads(k))
            half.append(dot(q4[n], k, 1, 1))
        weights, slopes, attended = [], [], []
        for n in n_all:
            seen = causal & (key_lane < fills[n])
            ws, ss, parts = [], [], []
            for h in range(H):
                s = half[n][h * length : (h + 1) * length, :]
                up = jnp.where(seen, jnp.tanh(s) + 1.0, 0.0)
                act = s * up
                ws.append(act.astype(BF16))
                ss.append(up * ((s - act) + (s + 1.0)))
                value = spread[rows[n], width + h * head : width + (h + 1) * head]
                parts.append(dot(ws[h], value))
            weights.append(ws)
            slopes.append(ss)
            attended.append(jnp.concatenate(parts, axis=1))
        shifted = [a - jnp.mean(a, axis=1, keepdims=True) for a in attended]
        scale = [lax.rsqrt(jnp.mean(a * a, axis=1, keepdims=True) + EPS) for a in shifted]
        dattended = []
        for n in n_all:
            normal = shifted[n] * scale[n]
            normals[n * length : (n + 1) * length, :] = normal
            gate = spread[rows[n], :width].astype(F32)
            upper = dgated[rows[n], :].astype(F32)
            dnormal = upper * gate
            spread[rows[n], :width] = (upper * normal).astype(BF16)
            where = jnp.maximum(fills[n] - 1, 0)
            last[pl.ds(blocks[n], 1), :] = normals[pl.ds(n * length + where, 1), :]
            mean = jnp.mean(dnormal, axis=1, keepdims=True)
            along = jnp.mean(dnormal * normal, axis=1, keepdims=True)
            dattended.append((scale[n] * (dnormal - mean - normal * along)).astype(BF16))
        dscores = []
        for n in n_all:
            ds = []
            for h in range(H):
                part = slice(h * head, (h + 1) * head)
                there = slice(width + h * head, width + (h + 1) * head)
                dweight = dot(dattended[n][:, part], spread[rows[n], there], 1, 1)
                ds.append((dweight * slopes[n][h]).astype(BF16))
                spread[rows[n], there] = dot(weights[n][h], dattended[n][:, part], 0, 0).astype(BF16)
            dscores.append(ds)
        for n in n_all:
            spread[rows[n], 2 * width : 2 * width + query] = dot(
                jnp.concatenate(dscores[n], axis=1), k4[n]
            ).astype(BF16)
            spread[rows[n], 2 * width + query : cols] = dot(
                jnp.concatenate(dscores[n], axis=0), q4[n], 0, 0
            ).astype(BF16)
        return carry

    lax.fori_loop(0, block_count // group, step, 0)


def write_letters(fills_ref, dest_ref, slot_ref, rows_ref, w_out_ref, proj, last, message):
    block_count, length = slot_ref.shape
    unique, width = rows_ref.shape
    fills = fills_ref[...]
    fill_col = column_of(fills.astype(F32)).astype(jnp.int32)
    last_slot = jnp.sum(
        jnp.where(iota((block_count, length), 1) == fill_col - 1, slot_ref[...].astype(F32), 0.0),
        axis=1,
        keepdims=True,
    ).astype(jnp.int32)
    pick = onehot(iota((block_count, unique), 1) == last_slot)
    gated = (last[...] * dot(pick, proj[:, :width])).astype(BF16)
    summary = (dot(pick, rows_ref[...]) + dot(gated, w_out_ref[...])).astype(BF16)
    row = iota((message.shape[0], block_count), 0)
    chosen = (row // PACK == dest_ref[...]) & (fills > 0)
    flag = jnp.sum(
        jnp.where(chosen & (row % PACK == width // LANES), 1.0, 0.0), axis=1, keepdims=True
    )
    letter = jnp.broadcast_to(flag, message.shape)
    for i in range(width // LANES):
        letter = letter + dot(
            onehot(chosen & (row % PACK == i)), summary[:, i * LANES : (i + 1) * LANES]
        )
    message[...] = letter.astype(BF16)


def read_letters(letters, summary_ref):
    rows = letters.shape[0]
    work, width = summary_ref.shape
    row, col = iota((rows, rows), 0), iota((rows, rows), 1)
    flag_col = col % PACK == width // LANES
    rank = dot(onehot(flag_col & (col // PACK < row // PACK)), letters[...])
    present = dot(onehot(flag_col & (col // PACK == row // PACK)), letters[...])
    wanted = (present > 0.5) & (rank.astype(jnp.int32) == iota((rows, LANES), 1))
    kind = iota((rows, LANES), 0) % PACK
    for i in range(width // LANES):
        part = dot(onehot(wanted & (kind == i)), letters[...], 0, 0)
        summary_ref[:, i * LANES : (i + 1) * LANES] = part[:work, :].astype(BF16)


def finish(w_in_ref, gain_in_ref, tall, spread, slope, hat, inv, dproj, grads):
    unique, width = hat.shape
    cols = slope.shape[1]
    parts, part_width = grads.shape[0], grads.shape[2]
    tile = min(FINISH_ROWS, unique)
    for r in range(0, unique, tile):
        rows = slice(r, r + tile)
        for c in range(0, cols, width):
            total = dot(tall[rows, :], spread[:, c : c + width])
            dproj[:, c : c + width] = (total * slope[rows, c : c + width]).astype(BF16)
        straight = dot(tall[rows, :], spread[:, cols:])
        dhat = dot(dproj[...], w_in_ref[...], 1, 1) * gain_in_ref[...]
        normal = hat[rows, :]
        scale = inv[rows, :1]
        mean = jnp.mean(dhat, axis=1, keepdims=True)
        along = jnp.mean(dhat * normal, axis=1, keepdims=True)
        dx = (scale * (dhat - mean - normal * along) + straight).astype(BF16)
        for p in range(parts):
            grads[p, rows, :] = dx[:, p * part_width : (p + 1) * part_width]


def step_kernel(
    dp_count,
    fill_ref, ids_ref, slot_ref, fills_ref, dest_ref, gain_in_ref, gain_out_ref,
    table_ref, aims_ref, w_in_hbm, w_out_hbm,
    summary_ref, total_ref,
    table_v, w_in_ref, w_out_ref, order, local, picks, picks_in, sorted_rows, served, rows_ref,
    here, tall, spread, dgated, proj, slope, hat, inv, normals, last, dproj,
    message, letters, grads, home, ordered, arrived,
    table_sem, load_sem, row_sems, pick_sems, letter_sems, home_sems, total_sems,
):
    table_count, cap = ids_ref.shape
    shard_rows, width = table_ref.shape
    cols = w_in_ref.shape[1]
    unique = table_count * cap
    run = shard_rows // dp_count
    length = slot_ref.shape[1]
    group = min(8, dp_count)
    span, part = group * run, group * 2 * table_count
    loads = [
        pltpu.make_async_copy(
            table_ref.at[pl.ds(g * span, span)], table_v.at[pl.ds(g * span, span)], table_sem.at[g]
        )
        for g in range(dp_count // group)
    ]
    w_out_load = pltpu.make_async_copy(w_out_hbm, w_out_ref, load_sem.at[0])
    aims_load = pltpu.make_async_copy(
        aims_ref, spread.at[:, pl.ds(cols, width)], load_sem.at[1]
    )
    w_in_load = pltpu.make_async_copy(w_in_hbm, w_in_ref, load_sem.at[2])
    for load in loads:
        load.start()
    barrier = pltpu.get_barrier_semaphore()
    greet(barrier, dp_count, table_count)

    def pair(sems):
        return sems.at[0], sems.at[1]

    fill_order(ids_ref, order, local, run)
    index = dot(order[...], local[...], 0, 0)
    picks[...] = onehot(index.astype(jnp.int32) == iota((unique, run), 1))
    for g, load in enumerate(loads):
        mine = picks[g * part : (g + 1) * part, :]
        wide = jnp.concatenate([mine] * group, axis=1)
        same = iota((part, span), 0) // (2 * table_count) == iota((part, span), 1) // run
        load.wait()
        if g == max(0, len(loads) - 2):
            for later in (w_out_load, aims_load, w_in_load):
                later.start()
        sorted_rows[g * part : (g + 1) * part, :] = dot(
            jnp.where(same, wide, jnp.zeros_like(wide)), table_v[g * span : (g + 1) * span, :]
        ).astype(BF16)
    served[...] = dot(order[...], sorted_rows[...]).astype(BF16)
    pl.semaphore_wait(barrier, dp_count + table_count - 2)
    row_exchange = Exchange("table", table_count, served, rows_ref, cap, pair(row_sems))
    row_exchange.start()
    pick_exchange = Exchange("dp", dp_count, picks, picks_in, 2 * table_count, pair(pick_sems))
    pick_exchange.start()

    prepare(slot_ref, here, tall)
    w_out_load.wait()
    aims_load.wait()
    weigh(fill_ref, length, w_out_ref, spread, dgated)
    w_in_load.wait()
    row_exchange.wait_recv()
    project(rows_ref, w_in_ref, gain_in_ref, gain_out_ref, length, proj, slope, hat, inv)
    gather(here, proj, spread)
    attend(fill_ref, length, spread, dgated, normals, last)
    write_letters(fills_ref, dest_ref, slot_ref, rows_ref, w_out_ref, proj, last, message)
    letter_exchange = Exchange("dp", dp_count, message, letters, PACK, pair(letter_sems))
    letter_exchange.start()
    finish(w_in_ref, gain_in_ref, tall, spread, slope, hat, inv, dproj, grads)

    parts = grads.shape[0]
    part_width = width // parts
    homes, totals = [], []
    for p in range(parts):
        homes.append(
            Exchange("table", table_count, grads.at[p], home.at[p], cap, pair(home_sems.at[p]))
        )
        totals.append(
            Exchange(
                "dp", dp_count, ordered.at[p], arrived.at[p], 2 * table_count, pair(total_sems.at[p])
            )
        )
        homes[p].start()
    for p in range(parts):
        homes[p].wait_recv()
        ordered[p, :, :] = dot(order[...], home[p, :, :], 0, 0).astype(BF16)
        totals[p].start()
    letter_exchange.wait_recv()
    read_letters(letters, summary_ref)
    pick_exchange.wait_recv()
    for p in range(parts):
        totals[p].wait_recv()
        total_ref[:, p * part_width : (p + 1) * part_width] = dot(
            picks_in[...], arrived[p, :, :], 0, 0
        )
    for exchange in [row_exchange, pick_exchange, letter_exchange] + homes + totals:
        exchange.wait_send()


def whole(space=pltpu.VMEM):
    return pl.BlockSpec(memory_space=space)


def body(
    embedding_table, served_ids, event_slot, block_fill, destination, target, w_in, w_out,
    gain_in, gain_out,
):
    dp_count, table_count = lax.axis_size("dp"), lax.axis_size("table")
    shard_rows, width = embedding_table.shape
    ids = served_ids[0, 0]
    cap = ids.shape[1]
    unique = table_count * cap
    run = shard_rows // dp_count
    slots = event_slot[0, 0]
    block_count, length = slots.shape
    work_count = block_count // 2
    events = block_count * length
    cols = w_in.shape[1]
    parts, part_width = PARTS, width // PARTS
    dma = pltpu.SemaphoreType.DMA
    vmem = pltpu.VMEM
    fills = block_fill[0, 0]
    summary, total = pl.pallas_call(
        functools.partial(step_kernel, dp_count),
        out_shape=(
            jax.ShapeDtypeStruct((work_count, width), BF16),
            jax.ShapeDtypeStruct((run, width), F32),
        ),
        in_specs=[whole(pltpu.SMEM)] + [whole()] * 6 + [whole(pl.ANY)] * 4,
        out_specs=(whole(), whole()),
        scratch_shapes=[
            vmem((shard_rows, width), BF16),
            vmem((width, cols), BF16),
            vmem((width, width), BF16),
            vmem((unique, unique), BF16),
            vmem((unique, run), BF16),
            vmem((unique, run), BF16),
            vmem((unique, run), BF16),
            vmem((unique, width), BF16),
            vmem((unique, width), BF16),
            vmem((unique, width), BF16),
        ]
        + compute_scratch(unique, events, cols, width, block_count, length)
        + [
            vmem((dp_count * PACK, LANES), BF16),
            vmem((dp_count * PACK, LANES), BF16),
            vmem((parts, unique, part_width), BF16),
            vmem((parts, unique, part_width), BF16),
            vmem((parts, unique, part_width), BF16),
            vmem((parts, unique, part_width), BF16),
            dma((max(1, dp_count // 8),)),
            dma((3,)),
            dma((2, table_count)),
            dma((2, dp_count)),
            dma((2, dp_count)),
            dma((parts, 2, table_count)),
            dma((parts, 2, dp_count)),
        ],
        compiler_params=pltpu.CompilerParams(
            vmem_limit_bytes=VMEM_BYTES, collective_id=0, has_side_effects=True
        ),
        name="step",
    )(
        fills, ids, slots, fills.reshape(1, -1), destination[0, 0].reshape(1, -1),
        gain_in.reshape(1, -1), gain_out.reshape(1, -1),
        embedding_table, target.reshape(events, width), w_in, w_out,
    )
    return (summary.reshape(1, 1, work_count, width), total.reshape(1, run, width))


def compute_scratch(unique, events, cols, width, block_count, length):
    vmem = pltpu.VMEM
    return [
        vmem((events, unique), BF16),
        vmem((unique, events), BF16),
        vmem((events, cols + width), BF16),
        vmem((events, width), BF16),
        vmem((unique, cols), BF16),
        vmem((unique, cols), F32),
        vmem((unique, width), F32),
        vmem((unique, LANES), F32),
        vmem((BLOCK_GROUP * length, width), F32),
        vmem((block_count, width), F32),
        vmem((min(FINISH_ROWS, unique), cols), BF16),
    ]


def solution(mesh):
    return jax.shard_map(
        body,
        mesh=mesh,
        in_specs=(
            P("table", None),
            P("dp", "table", None, None),
            P("dp", "table", None, None),
            P("dp", "table", None),
            P("dp", "table", None),
            P("dp", "table", None, None, None),
            P(), P(), P(), P(),
        ),
        out_specs=(P("dp", "table", None, None), P("table", "dp", None)),
        check_vma=False,
    )
```

```python
import functools

import jax
import jax.numpy as jnp
from jax import lax
from jax.experimental import pallas as pl
from jax.experimental.pallas import tpu as pltpu
from jax.sharding import PartitionSpec as P

H = 4
QK = 64
PACK = 16
LANES = 128
EPS = 1e-05
F32 = jnp.float32
BF16 = jnp.bfloat16
VMEM_BYTES = 60 * 1024 * 1024
PROJECT_ROWS = 256
GATHER_ROWS = 1024
BLOCK_GROUP = 4
PARTS = 2


def dot(a, b, ca=1, cb=0):
    return lax.dot_general(a, b, (((ca,), (cb,)), ((), ())), preferred_element_type=F32)


def iota(shape, axis):
    return lax.broadcasted_iota(jnp.int32, shape, axis)


def onehot(condition):
    return jnp.where(condition, 1.0, 0.0).astype(BF16)


def sigmoid(x):
    return 0.5 * jnp.tanh(0.5 * x) + 0.5


def column_of(row):
    n = row.shape[1]
    here = iota((n, n), 0) == iota((n, n), 1)
    return jnp.sum(jnp.where(here, row, 0.0), axis=1, keepdims=True)


def halved(slot, cap, unique):
    part = cap // 2
    return (slot % cap) // part * (unique // 2) + slot // cap * part + slot % part


def fill_order(ids_ref, order_ref, local_ref, run):
    table_count, cap = ids_ref.shape
    unique = table_count * cap
    for t in range(table_count):
        row = ids_ref[t : t + 1, :].astype(F32)
        column = column_of(row)
        rank = jnp.sum(jnp.where(row < column, 1.0, 0.0), axis=1, keepdims=True).astype(jnp.int32)
        place = (rank // 2) * (2 * table_count) + 2 * t + rank % 2
        hot = onehot(iota((cap, unique), 1) == place)
        local = (column.astype(jnp.int32) % run).astype(F32)
        local = jnp.broadcast_to(local, (cap, run)).astype(BF16)
        part = cap // 2
        for half in range(2):
            there = half * (unique // 2) + t * part
            here = slice(half * part, (half + 1) * part)
            order_ref[there : there + part, :] = hot[here, :]
            local_ref[there : there + part, :] = local[here, :]


def greet(barrier, dp_count, table_count):
    me_d, me_t = lax.axis_index("dp"), lax.axis_index("table")

    def signal_dp(step, carry):
        pl.semaphore_signal(barrier, inc=1, device_id={"dp": (me_d + step) % dp_count})
        return carry

    lax.fori_loop(1, dp_count, signal_dp, 0)
    for step in range(1, table_count):
        pl.semaphore_signal(barrier, inc=1, device_id={"table": (me_t + step) % table_count})


class Exchange:
    def __init__(self, axis, count, source, target, block, sems):
        self.axis, self.count, self.block = axis, count, block
        self.source, self.target = source, target
        self.send, self.recv = sems
        self.me = lax.axis_index(axis)

    def rows(self, index):
        return pl.ds(pl.multiple_of(index * self.block, self.block), self.block)

    def copy(self, peer, slot):
        return pltpu.make_async_remote_copy(
            src_ref=self.source.at[self.rows(peer)],
            dst_ref=self.target.at[self.rows(slot)],
            send_sem=self.send.at[peer],
            recv_sem=self.recv.at[slot],
            device_id={self.axis: peer},
        )

    def loop(self, step_fn):
        def step(index, carry):
            step_fn((self.me + index) % self.count)
            return carry

        lax.fori_loop(1, self.count, step, 0)

    def start(self):
        self.loop(lambda peer: self.copy(peer, self.me).start())
        self.target[self.rows(self.me), :] = self.source[self.rows(self.me), :]

    def wait_recv(self):
        self.loop(lambda peer: self.copy(peer, peer).wait_recv())

    def wait_send(self):
        self.loop(lambda peer: self.copy(peer, self.me).wait_send())


def prepare(slot_ref, here, tall):
    block_count, length = slot_ref.shape
    unique = here.shape[1]
    eye = iota((length, length), 0) == iota((length, length), 1)

    def one(b, carry):
        rows = pl.ds(pl.multiple_of(b * length, length), length)
        slot_row = slot_ref[pl.ds(b, 1), :]
        slot_col = jnp.sum(
            jnp.where(eye, slot_row.astype(F32), 0.0), axis=1, keepdims=True
        ).astype(jnp.int32)
        here[rows, :] = onehot(iota((length, unique), 1) == slot_col)
        tall[:, rows] = onehot(iota((unique, length), 0) == slot_row)
        return carry

    lax.fori_loop(0, block_count, one, 0)


def weigh(fill_ref, length, w_out_ref, spread, dgated):
    events, width = dgated.shape
    cols = spread.shape[1] - width
    position = iota((length, 1), 0)

    def one(b, carry):
        rows = pl.ds(pl.multiple_of(b * length, length), length)
        aim = spread[rows, cols:]
        live_aim = jnp.where(position < fill_ref[b], aim, jnp.zeros_like(aim))
        spread[rows, cols:] = live_aim
        dgated[rows, :] = dot(live_aim, w_out_ref[...], 1, 1).astype(BF16)
        return carry

    lax.fori_loop(0, events // length, one, 0)


def project(half, rows_ref, w_in_ref, gain_in_ref, gain_out_ref, length, proj, slope, hat, inv):
    unique, width = rows_ref.shape
    unique //= 2
    query = H * QK
    gain_in = gain_in_ref[...]
    tilt = 0.5 * QK ** (-0.5)
    lane = iota((1, 2 * query), 1)
    factors = [gain_out_ref[...], 1.0 / length, jnp.where(lane < query, tilt, 1.0)]
    chunk = min(PROJECT_ROWS, unique)

    def step(i, carry):
        rows = pl.ds(pl.multiple_of(half * unique + i * chunk, chunk), chunk)
        x = rows_ref[rows, :].astype(F32)
        shifted = x - jnp.mean(x, axis=1, keepdims=True)
        scale = lax.rsqrt(jnp.mean(shifted * shifted, axis=1, keepdims=True) + EPS)
        normal = shifted * scale
        hat[rows, :] = normal
        inv[rows, :] = jnp.broadcast_to(scale, (chunk, LANES))
        normed = (normal * gain_in).astype(BF16)
        for c, factor in enumerate(factors):
            part = slice(c * width, (c + 1) * width)
            pre = dot(normed, w_in_ref[:, part])
            sig = sigmoid(pre)
            act = pre * sig
            proj[rows, part] = (act * factor).astype(BF16)
            slope[rows, part] = (sig + act * (1.0 - sig)) * factor
        return carry

    lax.fori_loop(0, unique // chunk, step, 0)


def gather(here, proj, spread):
    events = here.shape[0]
    cols = proj.shape[1]
    chunk = min(GATHER_ROWS, events)
    width = cols // 3

    def step(i, carry):
        rows = pl.ds(pl.multiple_of(i * chunk, chunk), chunk)
        for c in range(0, cols, width):
            spread[rows, c : c + width] = dot(here[rows, :], proj[:, c : c + width]).astype(BF16)
        return carry

    lax.fori_loop(0, events // chunk, step, 0)


def attend(fill_ref, length, spread, dgated, normals, last):
    events, width = dgated.shape
    query = H * QK
    cols = 2 * width + 2 * query
    head = width // H
    block_count = events // length
    group = min(BLOCK_GROUP, block_count)
    causal = iota((length, length), 0) >= iota((length, length), 1)
    key_lane = iota((length, length), 1)
    low = iota((length, LANES), 1) < QK

    def heads(x):
        zero = jnp.zeros((length, LANES), BF16)
        parts = []
        for h in range(H):
            side = h // 2
            mine = x[:, side * LANES : (side + 1) * LANES]
            mine = jnp.where(low if h % 2 == 0 else ~low, mine, zero)
            parts.append(jnp.concatenate([mine, zero] if side == 0 else [zero, mine], axis=1))
        return jnp.concatenate(parts, axis=0)

    def step(i, carry):
        blocks = [group * i + n for n in range(group)]
        rows = [pl.ds(pl.multiple_of(b * length, length), length) for b in blocks]
        fills = [fill_ref[b] for b in blocks]
        n_all = range(group)
        q4, k4, half = [], [], []
        for n in n_all:
            q = spread[rows[n], 2 * width : 2 * width + query]
            k = spread[rows[n], 2 * width + query : cols]
            q4.append(heads(q))
            k4.append(heads(k))
            half.append(dot(q4[n], k, 1, 1))
        weights, slopes, attended = [], [], []
        for n in n_all:
            seen = causal & (key_lane < fills[n])
            ws, ss, parts = [], [], []
            for h in range(H):
                s = half[n][h * length : (h + 1) * length, :]
                up = jnp.where(seen, jnp.tanh(s) + 1.0, 0.0)
                act = s * up
                ws.append(act.astype(BF16))
                ss.append(up * ((s - act) + (s + 1.0)))
                value = spread[rows[n], width + h * head : width + (h + 1) * head]
                parts.append(dot(ws[h], value))
            weights.append(ws)
            slopes.append(ss)
            attended.append(jnp.concatenate(parts, axis=1))
        shifted = [a - jnp.mean(a, axis=1, keepdims=True) for a in attended]
        scale = [lax.rsqrt(jnp.mean(a * a, axis=1, keepdims=True) + EPS) for a in shifted]
        dattended = []
        for n in n_all:
            normal = shifted[n] * scale[n]
            normals[n * length : (n + 1) * length, :] = normal
            gate = spread[rows[n], :width].astype(F32)
            upper = dgated[rows[n], :].astype(F32)
            dnormal = upper * gate
            spread[rows[n], :width] = (upper * normal).astype(BF16)
            where = jnp.maximum(fills[n] - 1, 0)
            last[pl.ds(blocks[n], 1), :] = normals[pl.ds(n * length + where, 1), :]
            mean = jnp.mean(dnormal, axis=1, keepdims=True)
            along = jnp.mean(dnormal * normal, axis=1, keepdims=True)
            dattended.append((scale[n] * (dnormal - mean - normal * along)).astype(BF16))
        dscores = []
        for n in n_all:
            ds = []
            for h in range(H):
                part = slice(h * head, (h + 1) * head)
                there = slice(width + h * head, width + (h + 1) * head)
                dweight = dot(dattended[n][:, part], spread[rows[n], there], 1, 1)
                ds.append((dweight * slopes[n][h]).astype(BF16))
                spread[rows[n], there] = dot(weights[n][h], dattended[n][:, part], 0, 0).astype(BF16)
            dscores.append(ds)
        for n in n_all:
            spread[rows[n], 2 * width : 2 * width + query] = dot(
                jnp.concatenate(dscores[n], axis=1), k4[n]
            ).astype(BF16)
            spread[rows[n], 2 * width + query : cols] = dot(
                jnp.concatenate(dscores[n], axis=0), q4[n], 0, 0
            ).astype(BF16)
        return carry

    lax.fori_loop(0, block_count // group, step, 0)


def address_letters(fills_ref, dest_ref, marks, pick, chosen, flag):
    block_count, length = marks.shape
    unique = pick.shape[1]
    kinds = chosen.shape[0]
    fills = fills_ref[...]
    fill_col = column_of(fills.astype(F32)).astype(jnp.int32)
    last_mark = jnp.sum(
        jnp.where(iota((block_count, length), 1) == fill_col - 1, marks[...].astype(F32), 0.0),
        axis=1,
        keepdims=True,
    ).astype(jnp.int32)
    pick[...] = onehot(iota((block_count, unique), 1) == last_mark)
    row = iota((flag.shape[0], block_count), 0)
    mine = (row // PACK == dest_ref[...]) & (fills > 0)
    present = jnp.sum(jnp.where(mine & (row % PACK == kinds), 1.0, 0.0), axis=1, keepdims=True)
    flag[...] = jnp.broadcast_to(present, flag.shape).astype(BF16)
    for i in range(kinds):
        chosen[i, :, :] = onehot(mine & (row % PACK == i))


def write_letters(rows_ref, w_out_ref, proj, last, pick, chosen, flag, message):
    width = rows_ref.shape[1]
    gated = (last[...] * dot(pick[...], proj[:, :width])).astype(BF16)
    summary = (dot(pick[...], rows_ref[...]) + dot(gated, w_out_ref[...])).astype(BF16)
    letter = flag[...].astype(F32)
    for i in range(chosen.shape[0]):
        letter = letter + dot(chosen[i, :, :], summary[:, i * LANES : (i + 1) * LANES])
    message[...] = letter.astype(BF16)


def read_letters(letters, summary_ref):
    rows = letters.shape[0]
    work, width = summary_ref.shape
    row, col = iota((rows, rows), 0), iota((rows, rows), 1)
    flag_col = col % PACK == width // LANES
    rank = dot(onehot(flag_col & (col // PACK < row // PACK)), letters[...])
    present = dot(onehot(flag_col & (col // PACK == row // PACK)), letters[...])
    wanted = (present > 0.5) & (rank.astype(jnp.int32) == iota((rows, LANES), 1))
    kind = iota((rows, LANES), 0) % PACK
    for i in range(width // LANES):
        part = dot(onehot(wanted & (kind == i)), letters[...], 0, 0)
        summary_ref[:, i * LANES : (i + 1) * LANES] = part[:work, :].astype(BF16)


def finish(half, w_in_ref, gain_in_ref, tall, spread, slope, hat, inv, dproj, grads):
    unique, width = hat.shape
    cols = slope.shape[1]
    parts, part_width = grads.shape[0], grads.shape[2]
    tile = unique // 2
    rows = slice(half * tile, (half + 1) * tile)
    for c in range(0, cols, width):
        total = dot(tall[rows, :], spread[:, c : c + width])
        dproj[:, c : c + width] = (total * slope[rows, c : c + width]).astype(BF16)
    straight = dot(tall[rows, :], spread[:, cols:])
    dhat = dot(dproj[...], w_in_ref[...], 1, 1) * gain_in_ref[...]
    normal = hat[rows, :]
    scale = inv[rows, :1]
    mean = jnp.mean(dhat, axis=1, keepdims=True)
    along = jnp.mean(dhat * normal, axis=1, keepdims=True)
    dx = (scale * (dhat - mean - normal * along) + straight).astype(BF16)
    for p in range(parts):
        grads[p, rows, :] = dx[:, p * part_width : (p + 1) * part_width]


def step_kernel(
    dp_count,
    fill_ref, ids_ref, slot_ref, fills_ref, dest_ref, gain_in_ref, gain_out_ref,
    table_ref, aims_ref, w_in_hbm, w_out_hbm,
    summary_ref, total_ref,
    table_v, w_in_ref, w_out_ref, order, local, picks, picks_in, sorted_rows, served, rows_ref,
    here, tall, spread, dgated, proj, slope, hat, inv, normals, last, dproj,
    marks, pick, chosen, flag, message, letters, grads, home, ordered, arrived,
    table_sem, load_sem, row_sems, pick_sems, letter_sems, home_sems, total_sems,
):
    table_count, cap = ids_ref.shape
    shard_rows, width = table_ref.shape
    cols = w_in_ref.shape[1]
    unique = table_count * cap
    run = shard_rows // dp_count
    length = slot_ref.shape[1]
    group = min(8, dp_count)
    span, part = group * run, group * 2 * table_count
    loads = [
        pltpu.make_async_copy(
            table_ref.at[pl.ds(g * span, span)], table_v.at[pl.ds(g * span, span)], table_sem.at[g]
        )
        for g in range(dp_count // group)
    ]
    w_out_load = pltpu.make_async_copy(w_out_hbm, w_out_ref, load_sem.at[0])
    aims_load = pltpu.make_async_copy(
        aims_ref, spread.at[:, pl.ds(cols, width)], load_sem.at[1]
    )
    w_in_load = pltpu.make_async_copy(w_in_hbm, w_in_ref, load_sem.at[2])
    for load in loads:
        load.start()
    barrier = pltpu.get_barrier_semaphore()
    greet(barrier, dp_count, table_count)

    def pair(sems):
        return sems.at[0], sems.at[1]

    fill_order(ids_ref, order, local, run)
    index = dot(order[...], local[...], 0, 0)
    picks[...] = onehot(index.astype(jnp.int32) == iota((unique, run), 1))
    for g, load in enumerate(loads):
        mine = picks[g * part : (g + 1) * part, :]
        wide = jnp.concatenate([mine] * group, axis=1)
        same = iota((part, span), 0) // (2 * table_count) == iota((part, span), 1) // run
        load.wait()
        if g == max(0, len(loads) - 2):
            for later in (w_out_load, aims_load, w_in_load):
                later.start()
        sorted_rows[g * part : (g + 1) * part, :] = dot(
            jnp.where(same, wide, jnp.zeros_like(wide)), table_v[g * span : (g + 1) * span, :]
        ).astype(BF16)
    served[...] = dot(order[...], sorted_rows[...]).astype(BF16)
    pl.semaphore_wait(barrier, dp_count + table_count - 2)
    halves = [pl.ds(half * (unique // 2), unique // 2) for half in range(2)]
    row_exchanges = [
        Exchange(
            "table", table_count, served.at[rows], rows_ref.at[rows], cap // 2, pair(row_sems.at[half])
        )
        for half, rows in enumerate(halves)
    ]
    for exchange in row_exchanges:
        exchange.start()
    pick_exchange = Exchange("dp", dp_count, picks, picks_in, 2 * table_count, pair(pick_sems))
    pick_exchange.start()

    marks[...] = halved(slot_ref[...], cap, unique)
    prepare(marks, here, tall)
    address_letters(fills_ref, dest_ref, marks, pick, chosen, flag)
    w_out_load.wait()
    aims_load.wait()
    weigh(fill_ref, length, w_out_ref, spread, dgated)
    w_in_load.wait()
    for half, exchange in enumerate(row_exchanges):
        exchange.wait_recv()
        project(
            half, rows_ref, w_in_ref, gain_in_ref, gain_out_ref, length, proj, slope, hat, inv
        )
    gather(here, proj, spread)
    attend(fill_ref, length, spread, dgated, normals, last)
    write_letters(rows_ref, w_out_ref, proj, last, pick, chosen, flag, message)

    parts = grads.shape[0]
    part_width = width // parts
    letter_exchange = Exchange("dp", dp_count, message, letters, PACK, pair(letter_sems))
    homes, totals = [], []
    for half, rows in enumerate(halves):
        finish(half, w_in_ref, gain_in_ref, tall, spread, slope, hat, inv, dproj, grads)
        for p in range(parts):
            home_exchange = Exchange(
                "table", table_count, grads.at[p, rows], home.at[p, rows], cap // 2,
                pair(home_sems.at[half, p]),
            )
            home_exchange.start()
            homes.append(home_exchange)
        if half == 0:
            letter_exchange.start()
    for p in range(parts):
        homes[p].wait_recv()
        homes[parts + p].wait_recv()
        ordered[p, :, :] = dot(order[...], home[p, :, :], 0, 0).astype(BF16)
        totals.append(
            Exchange(
                "dp", dp_count, ordered.at[p], arrived.at[p], 2 * table_count, pair(total_sems.at[p])
            )
        )
        totals[p].start()
    letter_exchange.wait_recv()
    read_letters(letters, summary_ref)
    pick_exchange.wait_recv()
    for p in range(parts):
        totals[p].wait_recv()
        total_ref[:, p * part_width : (p + 1) * part_width] = dot(
            picks_in[...], arrived[p, :, :], 0, 0
        )
    for exchange in row_exchanges + [pick_exchange, letter_exchange] + homes + totals:
        exchange.wait_send()


def hand_on(summary_in, total_in, summary_out, total_out, sems):
    copies = [
        pltpu.make_async_copy(summary_in, summary_out, sems.at[0]),
        pltpu.make_async_copy(total_in, total_out, sems.at[1]),
    ]
    for copy in copies:
        copy.start()
    for copy in copies:
        copy.wait()


def whole(space=pltpu.VMEM):
    return pl.BlockSpec(memory_space=space)


def body(
    embedding_table, served_ids, event_slot, block_fill, destination, target, w_in, w_out,
    gain_in, gain_out,
):
    dp_count, table_count = lax.axis_size("dp"), lax.axis_size("table")
    shard_rows, width = embedding_table.shape
    ids = served_ids[0, 0]
    cap = ids.shape[1]
    unique = table_count * cap
    run = shard_rows // dp_count
    slots = event_slot[0, 0]
    block_count, length = slots.shape
    work_count = block_count // 2
    events = block_count * length
    cols = w_in.shape[1]
    parts, part_width = PARTS, width // PARTS
    dma = pltpu.SemaphoreType.DMA
    vmem = pltpu.VMEM
    fills = block_fill[0, 0]
    summary, total = pl.pallas_call(
        functools.partial(step_kernel, dp_count),
        out_shape=(
            jax.ShapeDtypeStruct((work_count, width), BF16),
            jax.ShapeDtypeStruct((run, width), F32),
        ),
        in_specs=[whole(pltpu.SMEM)] + [whole()] * 6 + [whole(pl.ANY)] * 4,
        out_specs=(whole(), whole()),
        scratch_shapes=[
            vmem((shard_rows, width), BF16),
            vmem((width, cols), BF16),
            vmem((width, width), BF16),
            vmem((unique, unique), BF16),
            vmem((unique, run), BF16),
            vmem((unique, run), BF16),
            vmem((unique, run), BF16),
            vmem((unique, width), BF16),
            vmem((unique, width), BF16),
            vmem((unique, width), BF16),
        ]
        + compute_scratch(unique, events, cols, width, block_count, length)
        + [
            vmem((block_count, length), jnp.int32),
            vmem((block_count, unique), BF16),
            vmem((width // LANES, dp_count * PACK, block_count), BF16),
            vmem((dp_count * PACK, LANES), BF16),
            vmem((dp_count * PACK, LANES), BF16),
            vmem((dp_count * PACK, LANES), BF16),
            vmem((parts, unique, part_width), BF16),
            vmem((parts, unique, part_width), BF16),
            vmem((parts, unique, part_width), BF16),
            vmem((parts, unique, part_width), BF16),
            dma((max(1, dp_count // 8),)),
            dma((3,)),
            dma((2, 2, table_count)),
            dma((2, dp_count)),
            dma((2, dp_count)),
            dma((2, parts, 2, table_count)),
            dma((parts, 2, dp_count)),
        ],
        compiler_params=pltpu.CompilerParams(
            vmem_limit_bytes=VMEM_BYTES, collective_id=0, has_side_effects=True
        ),
        name="step",
    )(
        fills, ids, slots, fills.reshape(1, -1), destination[0, 0].reshape(1, -1),
        gain_in.reshape(1, -1), gain_out.reshape(1, -1),
        embedding_table, target.reshape(events, width), w_in, w_out,
    )
    summary, total = pl.pallas_call(
        hand_on,
        out_shape=(
            jax.ShapeDtypeStruct((work_count, width), BF16),
            jax.ShapeDtypeStruct((run, width), F32),
        ),
        in_specs=[whole(pl.ANY)] * 2,
        out_specs=(whole(pl.ANY), whole(pl.ANY)),
        scratch_shapes=[dma((2,))],
        compiler_params=pltpu.CompilerParams(vmem_limit_bytes=VMEM_BYTES),
        name="hand_on",
    )(summary, total)
    return (summary.reshape(1, 1, work_count, width), total.reshape(1, run, width))


def compute_scratch(unique, events, cols, width, block_count, length):
    vmem = pltpu.VMEM
    return [
        vmem((events, unique), BF16),
        vmem((unique, events), BF16),
        vmem((events, cols + width), BF16),
        vmem((events, width), BF16),
        vmem((unique, cols), BF16),
        vmem((unique, cols), F32),
        vmem((unique, width), F32),
        vmem((unique, LANES), F32),
        vmem((BLOCK_GROUP * length, width), F32),
        vmem((block_count, width), F32),
        vmem((unique // 2, cols), BF16),
    ]


def solution(mesh):
    return jax.shard_map(
        body,
        mesh=mesh,
        in_specs=(
            P("table", None),
            P("dp", "table", None, None),
            P("dp", "table", None, None),
            P("dp", "table", None),
            P("dp", "table", None),
            P("dp", "table", None, None, None),
            P(), P(), P(), P(),
        ),
        out_specs=(P("dp", "table", None, None), P("table", "dp", None)),
        check_vma=False,
    )
```

```python
import functools

import jax
import jax.numpy as jnp
from jax import lax
from jax.experimental import pallas as pl
from jax.experimental.pallas import tpu as pltpu
from jax.sharding import PartitionSpec as P

H = 4
QK = 64
PACK = 16
LANES = 128
EPS = 1e-05
F32 = jnp.float32
BF16 = jnp.bfloat16
VMEM_BYTES = 60 * 1024 * 1024
PROJECT_ROWS = 256
GATHER_ROWS = 1024
BLOCK_GROUP = 4
PARTS = 1


def dot(a, b, ca=1, cb=0):
    return lax.dot_general(a, b, (((ca,), (cb,)), ((), ())), preferred_element_type=F32)


def iota(shape, axis):
    return lax.broadcasted_iota(jnp.int32, shape, axis)


def onehot(condition):
    return jnp.where(condition, 1.0, 0.0).astype(BF16)


def sigmoid(x):
    return 0.5 * jnp.tanh(0.5 * x) + 0.5


def column_of(row):
    n = row.shape[1]
    here = iota((n, n), 0) == iota((n, n), 1)
    return jnp.sum(jnp.where(here, row, 0.0), axis=1, keepdims=True)


def halved(slot, cap, unique):
    part = cap // 2
    return (slot % cap) // part * (unique // 2) + slot // cap * part + slot % part


def fill_order(ids_ref, order_ref, local_ref, run):
    table_count, cap = ids_ref.shape
    unique = table_count * cap
    for t in range(table_count):
        row = ids_ref[t : t + 1, :].astype(F32)
        column = column_of(row)
        rank = jnp.sum(jnp.where(row < column, 1.0, 0.0), axis=1, keepdims=True).astype(jnp.int32)
        place = (rank // 2) * (2 * table_count) + 2 * t + rank % 2
        hot = onehot(iota((cap, unique), 1) == place)
        local = (column.astype(jnp.int32) % run).astype(F32)
        local = jnp.broadcast_to(local, (cap, run)).astype(BF16)
        part = cap // 2
        for half in range(2):
            there = half * (unique // 2) + t * part
            here = slice(half * part, (half + 1) * part)
            order_ref[there : there + part, :] = hot[here, :]
            local_ref[there : there + part, :] = local[here, :]


def greet(barrier, dp_count, table_count):
    me_d, me_t = lax.axis_index("dp"), lax.axis_index("table")

    def signal_dp(step, carry):
        pl.semaphore_signal(barrier, inc=1, device_id={"dp": (me_d + step) % dp_count})
        return carry

    lax.fori_loop(1, dp_count, signal_dp, 0)
    for step in range(1, table_count):
        pl.semaphore_signal(barrier, inc=1, device_id={"table": (me_t + step) % table_count})


class Exchange:
    def __init__(self, axis, count, source, target, block, sems):
        self.axis, self.count, self.block = axis, count, block
        self.source, self.target = source, target
        self.send, self.recv = sems
        self.me = lax.axis_index(axis)

    def rows(self, index):
        return pl.ds(pl.multiple_of(index * self.block, self.block), self.block)

    def copy(self, peer, slot):
        return pltpu.make_async_remote_copy(
            src_ref=self.source.at[self.rows(peer)],
            dst_ref=self.target.at[self.rows(slot)],
            send_sem=self.send,
            recv_sem=self.recv,
            device_id={self.axis: peer},
        )

    def loop(self, step_fn):
        def step(index, carry):
            step_fn((self.me + index) % self.count)
            return carry

        lax.fori_loop(1, self.count, step, 0)

    def start(self):
        self.loop(lambda peer: self.copy(peer, self.me).start())
        self.target[self.rows(self.me), :] = self.source[self.rows(self.me), :]

    def wait(self, sem):
        rows = pl.ds(0, (self.count - 1) * self.block)
        pltpu.make_async_copy(self.source.at[rows], self.target.at[rows], sem).wait()

    def wait_recv(self):
        self.wait(self.recv)

    def wait_send(self):
        self.wait(self.send)


def prepare(slot_ref, here, tall):
    block_count, length = slot_ref.shape
    unique = here.shape[1]
    eye = iota((length, length), 0) == iota((length, length), 1)

    def one(b, carry):
        rows = pl.ds(pl.multiple_of(b * length, length), length)
        slot_row = slot_ref[pl.ds(b, 1), :]
        slot_col = jnp.sum(
            jnp.where(eye, slot_row.astype(F32), 0.0), axis=1, keepdims=True
        ).astype(jnp.int32)
        here[rows, :] = onehot(iota((length, unique), 1) == slot_col)
        tall[:, rows] = onehot(iota((unique, length), 0) == slot_row)
        return carry

    lax.fori_loop(0, block_count, one, 0)


def weigh(fill_ref, length, w_out_ref, spread, dgated):
    events, width = dgated.shape
    cols = spread.shape[1] - width
    position = iota((length, 1), 0)

    def one(b, carry):
        rows = pl.ds(pl.multiple_of(b * length, length), length)
        aim = spread[rows, cols:]
        live_aim = jnp.where(position < fill_ref[b], aim, jnp.zeros_like(aim))
        spread[rows, cols:] = live_aim
        dgated[rows, :] = dot(live_aim, w_out_ref[...], 1, 1).astype(BF16)
        return carry

    lax.fori_loop(0, events // length, one, 0)


def project(half, rows_ref, w_in_ref, gain_in_ref, gain_out_ref, length, proj, slope, hat, inv):
    unique, width = rows_ref.shape
    unique //= 2
    query = H * QK
    gain_in = gain_in_ref[...]
    tilt = 0.5 * QK ** (-0.5)
    lane = iota((1, 2 * query), 1)
    factors = [gain_out_ref[...], 1.0 / length, jnp.where(lane < query, tilt, 1.0)]
    chunk = min(PROJECT_ROWS, unique)

    def step(i, carry):
        rows = pl.ds(pl.multiple_of(half * unique + i * chunk, chunk), chunk)
        x = rows_ref[rows, :].astype(F32)
        shifted = x - jnp.mean(x, axis=1, keepdims=True)
        scale = lax.rsqrt(jnp.mean(shifted * shifted, axis=1, keepdims=True) + EPS)
        normal = shifted * scale
        hat[rows, :] = normal
        inv[rows, :] = jnp.broadcast_to(scale, (chunk, LANES))
        normed = (normal * gain_in).astype(BF16)
        for c, factor in enumerate(factors):
            part = slice(c * width, (c + 1) * width)
            pre = dot(normed, w_in_ref[:, part])
            sig = sigmoid(pre)
            act = pre * sig
            proj[rows, part] = (act * factor).astype(BF16)
            slope[rows, part] = (sig + act * (1.0 - sig)) * factor
        return carry

    lax.fori_loop(0, unique // chunk, step, 0)


def gather(here, proj, spread):
    events = here.shape[0]
    cols = proj.shape[1]
    chunk = min(GATHER_ROWS, events)
    width = cols // 3

    def step(i, carry):
        rows = pl.ds(pl.multiple_of(i * chunk, chunk), chunk)
        for c in range(0, cols, width):
            spread[rows, c : c + width] = dot(here[rows, :], proj[:, c : c + width]).astype(BF16)
        return carry

    lax.fori_loop(0, events // chunk, step, 0)


def attend(fill_ref, length, spread, dgated, normals, last):
    events, width = dgated.shape
    query = H * QK
    cols = 2 * width + 2 * query
    head = width // H
    block_count = events // length
    group = min(BLOCK_GROUP, block_count)
    causal = iota((length, length), 0) >= iota((length, length), 1)
    key_lane = iota((length, length), 1)
    low = iota((length, LANES), 1) < QK

    def heads(x):
        zero = jnp.zeros((length, LANES), BF16)
        parts = []
        for h in range(H):
            side = h // 2
            mine = x[:, side * LANES : (side + 1) * LANES]
            mine = jnp.where(low if h % 2 == 0 else ~low, mine, zero)
            parts.append(jnp.concatenate([mine, zero] if side == 0 else [zero, mine], axis=1))
        return jnp.concatenate(parts, axis=0)

    def step(i, carry):
        blocks = [group * i + n for n in range(group)]
        rows = [pl.ds(pl.multiple_of(b * length, length), length) for b in blocks]
        fills = [fill_ref[b] for b in blocks]
        n_all = range(group)
        q4, k4, half = [], [], []
        for n in n_all:
            q = spread[rows[n], 2 * width : 2 * width + query]
            k = spread[rows[n], 2 * width + query : cols]
            q4.append(heads(q))
            k4.append(heads(k))
            half.append(dot(q4[n], k, 1, 1))
        weights, slopes, attended = [], [], []
        for n in n_all:
            seen = causal & (key_lane < fills[n])
            ws, ss, parts = [], [], []
            for h in range(H):
                s = half[n][h * length : (h + 1) * length, :]
                up = jnp.where(seen, jnp.tanh(s) + 1.0, 0.0)
                act = s * up
                ws.append(act.astype(BF16))
                ss.append(up * ((s - act) + (s + 1.0)))
                value = spread[rows[n], width + h * head : width + (h + 1) * head]
                parts.append(dot(ws[h], value))
            weights.append(ws)
            slopes.append(ss)
            attended.append(jnp.concatenate(parts, axis=1))
        shifted = [a - jnp.mean(a, axis=1, keepdims=True) for a in attended]
        scale = [lax.rsqrt(jnp.mean(a * a, axis=1, keepdims=True) + EPS) for a in shifted]
        dattended = []
        for n in n_all:
            normal = shifted[n] * scale[n]
            normals[n * length : (n + 1) * length, :] = normal
            gate = spread[rows[n], :width].astype(F32)
            upper = dgated[rows[n], :].astype(F32)
            dnormal = upper * gate
            spread[rows[n], :width] = (upper * normal).astype(BF16)
            where = jnp.maximum(fills[n] - 1, 0)
            last[pl.ds(blocks[n], 1), :] = normals[pl.ds(n * length + where, 1), :]
            mean = jnp.mean(dnormal, axis=1, keepdims=True)
            along = jnp.mean(dnormal * normal, axis=1, keepdims=True)
            dattended.append((scale[n] * (dnormal - mean - normal * along)).astype(BF16))
        dscores = []
        for n in n_all:
            ds = []
            for h in range(H):
                part = slice(h * head, (h + 1) * head)
                there = slice(width + h * head, width + (h + 1) * head)
                dweight = dot(dattended[n][:, part], spread[rows[n], there], 1, 1)
                ds.append((dweight * slopes[n][h]).astype(BF16))
                spread[rows[n], there] = dot(weights[n][h], dattended[n][:, part], 0, 0).astype(BF16)
            dscores.append(ds)
        for n in n_all:
            spread[rows[n], 2 * width : 2 * width + query] = dot(
                jnp.concatenate(dscores[n], axis=1), k4[n]
            ).astype(BF16)
            spread[rows[n], 2 * width + query : cols] = dot(
                jnp.concatenate(dscores[n], axis=0), q4[n], 0, 0
            ).astype(BF16)
        return carry

    lax.fori_loop(0, block_count // group, step, 0)


def address_letters(fills_ref, dest_ref, marks, pick, chosen, flag):
    block_count, length = marks.shape
    unique = pick.shape[1]
    kinds = chosen.shape[0]
    fills = fills_ref[...]
    fill_col = column_of(fills.astype(F32)).astype(jnp.int32)
    last_mark = jnp.sum(
        jnp.where(iota((block_count, length), 1) == fill_col - 1, marks[...].astype(F32), 0.0),
        axis=1,
        keepdims=True,
    ).astype(jnp.int32)
    pick[...] = onehot(iota((block_count, unique), 1) == last_mark)
    row = iota((flag.shape[0], block_count), 0)
    mine = (row // PACK == dest_ref[...]) & (fills > 0)
    present = jnp.sum(jnp.where(mine & (row % PACK == kinds), 1.0, 0.0), axis=1, keepdims=True)
    flag[...] = jnp.broadcast_to(present, flag.shape).astype(BF16)
    for i in range(kinds):
        chosen[i, :, :] = onehot(mine & (row % PACK == i))


def write_letters(rows_ref, w_out_ref, proj, last, pick, chosen, flag, message):
    width = rows_ref.shape[1]
    gated = (last[...] * dot(pick[...], proj[:, :width])).astype(BF16)
    summary = (dot(pick[...], rows_ref[...]) + dot(gated, w_out_ref[...])).astype(BF16)
    letter = flag[...].astype(F32)
    for i in range(chosen.shape[0]):
        letter = letter + dot(chosen[i, :, :], summary[:, i * LANES : (i + 1) * LANES])
    message[...] = letter.astype(BF16)


def read_letters(letters, summary_ref):
    rows = letters.shape[0]
    work, width = summary_ref.shape
    row, col = iota((rows, rows), 0), iota((rows, rows), 1)
    flag_col = col % PACK == width // LANES
    rank = dot(onehot(flag_col & (col // PACK < row // PACK)), letters[...])
    present = dot(onehot(flag_col & (col // PACK == row // PACK)), letters[...])
    wanted = (present > 0.5) & (rank.astype(jnp.int32) == iota((rows, LANES), 1))
    kind = iota((rows, LANES), 0) % PACK
    for i in range(width // LANES):
        part = dot(onehot(wanted & (kind == i)), letters[...], 0, 0)
        summary_ref[:, i * LANES : (i + 1) * LANES] = part[:work, :].astype(BF16)


def finish(half, w_in_ref, gain_in_ref, tall, spread, slope, hat, inv, dproj, grads):
    unique, width = hat.shape
    cols = slope.shape[1]
    parts, part_width = grads.shape[0], grads.shape[2]
    tile = unique // 2
    rows = slice(half * tile, (half + 1) * tile)
    for c in range(0, cols, width):
        total = dot(tall[rows, :], spread[:, c : c + width])
        dproj[:, c : c + width] = (total * slope[rows, c : c + width]).astype(BF16)
    straight = dot(tall[rows, :], spread[:, cols:])
    dhat = dot(dproj[...], w_in_ref[...], 1, 1) * gain_in_ref[...]
    normal = hat[rows, :]
    scale = inv[rows, :1]
    mean = jnp.mean(dhat, axis=1, keepdims=True)
    along = jnp.mean(dhat * normal, axis=1, keepdims=True)
    dx = (scale * (dhat - mean - normal * along) + straight).astype(BF16)
    for p in range(parts):
        grads[p, rows, :] = dx[:, p * part_width : (p + 1) * part_width]


def step_kernel(
    dp_count,
    fill_ref, ids_ref, slot_ref, fills_ref, dest_ref, gain_in_ref, gain_out_ref,
    table_ref, aims_ref, w_in_hbm, w_out_hbm,
    summary_ref, total_ref,
    table_v, w_in_ref, w_out_ref, order, local, picks, picks_in, sorted_rows, served, rows_ref,
    here, tall, spread, dgated, proj, slope, hat, inv, normals, last, dproj,
    marks, pick, chosen, flag, message, letters, grads, home, ordered, arrived,
    table_sem, load_sem, row_sems, pick_sems, letter_sems, home_sems, total_sems,
):
    table_count, cap = ids_ref.shape
    shard_rows, width = table_ref.shape
    cols = w_in_ref.shape[1]
    unique = table_count * cap
    run = shard_rows // dp_count
    length = slot_ref.shape[1]
    group = min(8, dp_count)
    span, part = group * run, group * 2 * table_count
    loads = [
        pltpu.make_async_copy(
            table_ref.at[pl.ds(g * span, span)], table_v.at[pl.ds(g * span, span)], table_sem.at[g]
        )
        for g in range(dp_count // group)
    ]
    w_out_load = pltpu.make_async_copy(w_out_hbm, w_out_ref, load_sem.at[0])
    aims_load = pltpu.make_async_copy(
        aims_ref, spread.at[:, pl.ds(cols, width)], load_sem.at[1]
    )
    w_in_load = pltpu.make_async_copy(w_in_hbm, w_in_ref, load_sem.at[2])
    for load in loads:
        load.start()
    barrier = pltpu.get_barrier_semaphore()
    greet(barrier, dp_count, table_count)

    def pair(sems):
        return sems.at[0], sems.at[1]

    fill_order(ids_ref, order, local, run)
    index = dot(order[...], local[...], 0, 0)
    picks[...] = onehot(index.astype(jnp.int32) == iota((unique, run), 1))
    for g, load in enumerate(loads):
        mine = picks[g * part : (g + 1) * part, :]
        wide = jnp.concatenate([mine] * group, axis=1)
        same = iota((part, span), 0) // (2 * table_count) == iota((part, span), 1) // run
        load.wait()
        if g == max(0, len(loads) - 2):
            for later in (w_out_load, aims_load, w_in_load):
                later.start()
        sorted_rows[g * part : (g + 1) * part, :] = dot(
            jnp.where(same, wide, jnp.zeros_like(wide)), table_v[g * span : (g + 1) * span, :]
        ).astype(BF16)
    served[...] = dot(order[...], sorted_rows[...]).astype(BF16)
    pl.semaphore_wait(barrier, dp_count + table_count - 2)
    halves = [pl.ds(half * (unique // 2), unique // 2) for half in range(2)]
    row_exchanges = [
        Exchange(
            "table", table_count, served.at[rows], rows_ref.at[rows], cap // 2, pair(row_sems.at[half])
        )
        for half, rows in enumerate(halves)
    ]
    for exchange in row_exchanges:
        exchange.start()
    pick_exchange = Exchange("dp", dp_count, picks, picks_in, 2 * table_count, pair(pick_sems))
    pick_exchange.start()

    marks[...] = halved(slot_ref[...], cap, unique)
    prepare(marks, here, tall)
    address_letters(fills_ref, dest_ref, marks, pick, chosen, flag)
    w_out_load.wait()
    aims_load.wait()
    weigh(fill_ref, length, w_out_ref, spread, dgated)
    w_in_load.wait()
    for half, exchange in enumerate(row_exchanges):
        exchange.wait_recv()
        project(
            half, rows_ref, w_in_ref, gain_in_ref, gain_out_ref, length, proj, slope, hat, inv
        )
    gather(here, proj, spread)
    attend(fill_ref, length, spread, dgated, normals, last)
    write_letters(rows_ref, w_out_ref, proj, last, pick, chosen, flag, message)

    parts = grads.shape[0]
    part_width = width // parts
    letter_exchange = Exchange("dp", dp_count, message, letters, PACK, pair(letter_sems))
    homes, totals = [], []
    for half, rows in enumerate(halves):
        finish(half, w_in_ref, gain_in_ref, tall, spread, slope, hat, inv, dproj, grads)
        for p in range(parts):
            home_exchange = Exchange(
                "table", table_count, grads.at[p, rows], home.at[p, rows], cap // 2,
                pair(home_sems.at[half, p]),
            )
            home_exchange.start()
            homes.append(home_exchange)
        if half == 0:
            letter_exchange.start()
    for p in range(parts):
        homes[p].wait_recv()
        homes[parts + p].wait_recv()
        ordered[p, :, :] = dot(order[...], home[p, :, :], 0, 0).astype(BF16)
        totals.append(
            Exchange(
                "dp", dp_count, ordered.at[p], arrived.at[p], 2 * table_count, pair(total_sems.at[p])
            )
        )
        totals[p].start()
    letter_exchange.wait_recv()
    read_letters(letters, summary_ref)
    pick_exchange.wait_recv()
    for exchange in row_exchanges + [pick_exchange, letter_exchange] + homes:
        exchange.wait_send()
    for p in range(parts):
        totals[p].wait_recv()
        total_ref[:, p * part_width : (p + 1) * part_width] = dot(
            picks_in[...], arrived[p, :, :], 0, 0
        )
    for exchange in totals:
        exchange.wait_send()


def hand_on(summary_in, total_in, summary_out, total_out):
    summary_out[...] = summary_in[...]
    total_out[...] = total_in[...]


def whole(space=pltpu.VMEM):
    return pl.BlockSpec(memory_space=space)


def body(
    embedding_table, served_ids, event_slot, block_fill, destination, target, w_in, w_out,
    gain_in, gain_out,
):
    dp_count, table_count = lax.axis_size("dp"), lax.axis_size("table")
    shard_rows, width = embedding_table.shape
    ids = served_ids[0, 0]
    cap = ids.shape[1]
    unique = table_count * cap
    run = shard_rows // dp_count
    slots = event_slot[0, 0]
    block_count, length = slots.shape
    work_count = block_count // 2
    events = block_count * length
    cols = w_in.shape[1]
    parts, part_width = PARTS, width // PARTS
    dma = pltpu.SemaphoreType.DMA
    vmem = pltpu.VMEM
    fills = block_fill[0, 0]
    summary, total = pl.pallas_call(
        functools.partial(step_kernel, dp_count),
        out_shape=(
            jax.ShapeDtypeStruct((work_count, width), BF16),
            jax.ShapeDtypeStruct((run, width), F32),
        ),
        in_specs=[whole(pltpu.SMEM)] + [whole()] * 6 + [whole(pl.ANY)] * 4,
        out_specs=(whole(), whole()),
        scratch_shapes=[
            vmem((shard_rows, width), BF16),
            vmem((width, cols), BF16),
            vmem((width, width), BF16),
            vmem((unique, unique), BF16),
            vmem((unique, run), BF16),
            vmem((unique, run), BF16),
            vmem((unique, run), BF16),
            vmem((unique, width), BF16),
            vmem((unique, width), BF16),
            vmem((unique, width), BF16),
        ]
        + compute_scratch(unique, events, cols, width, block_count, length)
        + [
            vmem((block_count, length), jnp.int32),
            vmem((block_count, unique), BF16),
            vmem((width // LANES, dp_count * PACK, block_count), BF16),
            vmem((dp_count * PACK, LANES), BF16),
            vmem((dp_count * PACK, LANES), BF16),
            vmem((dp_count * PACK, LANES), BF16),
            vmem((parts, unique, part_width), BF16),
            vmem((parts, unique, part_width), BF16),
            vmem((parts, unique, part_width), BF16),
            vmem((parts, unique, part_width), BF16),
            dma((max(1, dp_count // 8),)),
            dma((3,)),
            dma((2, 2)),
            dma((2,)),
            dma((2,)),
            dma((2, parts, 2)),
            dma((parts, 2)),
        ],
        compiler_params=pltpu.CompilerParams(
            vmem_limit_bytes=VMEM_BYTES, collective_id=0, has_side_effects=True
        ),
        name="step",
    )(
        fills, ids, slots, fills.reshape(1, -1), destination[0, 0].reshape(1, -1),
        gain_in.reshape(1, -1), gain_out.reshape(1, -1),
        embedding_table, target.reshape(events, width), w_in, w_out,
    )
    summary, total = pl.pallas_call(
        hand_on,
        out_shape=(
            jax.ShapeDtypeStruct((work_count, width), BF16),
            jax.ShapeDtypeStruct((run, width), F32),
        ),
        in_specs=[whole()] * 2,
        out_specs=(whole(), whole()),
        compiler_params=pltpu.CompilerParams(vmem_limit_bytes=VMEM_BYTES),
        name="hand_on",
    )(summary, total)
    return (summary.reshape(1, 1, work_count, width), total.reshape(1, run, width))


def compute_scratch(unique, events, cols, width, block_count, length):
    vmem = pltpu.VMEM
    return [
        vmem((events, unique), BF16),
        vmem((unique, events), BF16),
        vmem((events, cols + width), BF16),
        vmem((events, width), BF16),
        vmem((unique, cols), BF16),
        vmem((unique, cols), F32),
        vmem((unique, width), F32),
        vmem((unique, LANES), F32),
        vmem((BLOCK_GROUP * length, width), F32),
        vmem((block_count, width), F32),
        vmem((unique // 2, cols), BF16),
    ]


def solution(mesh):
    return jax.shard_map(
        body,
        mesh=mesh,
        in_specs=(
            P("table", None),
            P("dp", "table", None, None),
            P("dp", "table", None, None),
            P("dp", "table", None),
            P("dp", "table", None),
            P("dp", "table", None, None, None),
            P(), P(), P(), P(),
        ),
        out_specs=(P("dp", "table", None, None), P("table", "dp", None)),
        check_vma=False,
    )
```

```python
import functools

import jax
import jax.numpy as jnp
from jax import lax
from jax.experimental import pallas as pl
from jax.experimental.pallas import tpu as pltpu
from jax.sharding import PartitionSpec as P

H = 4
QK = 64
PACK = 16
LANES = 128
EPS = 1e-05
F32 = jnp.float32
BF16 = jnp.bfloat16
VMEM_BYTES = 60 * 1024 * 1024
PROJECT_ROWS = 256
GATHER_ROWS = 1024
BLOCK_GROUP = 4


def dot(a, b, ca=1, cb=0):
    return lax.dot_general(a, b, (((ca,), (cb,)), ((), ())), preferred_element_type=F32)


def iota(shape, axis):
    return lax.broadcasted_iota(jnp.int32, shape, axis)


def onehot(condition):
    return jnp.where(condition, 1.0, 0.0).astype(BF16)


def sigmoid(x):
    return 0.5 * jnp.tanh(0.5 * x) + 0.5


def column_of(row):
    n = row.shape[1]
    here = iota((n, n), 0) == iota((n, n), 1)
    return jnp.sum(jnp.where(here, row, 0.0), axis=1, keepdims=True)


def to_halves(unique, table_count):
    part = unique // 2 // table_count
    row, col = iota((unique, unique), 0), iota((unique, unique), 1)
    half, t, place = row // (unique // 2), row // part % table_count, row % part
    return onehot(col == (place // 2 * 2 + half) * (2 * table_count) + 2 * t + place % 2)


def from_half(size, table_count):
    row, col = iota((size, size), 0), iota((size, size), 1)
    pack = 2 * table_count
    return onehot(col == row % pack // 2 * (size // table_count) + row // pack * 2 + row % 2)


def fill_order(ids_ref, order_ref, local_ref, label_ref, run):
    table_count, cap = ids_ref.shape
    unique = table_count * cap
    for t in range(table_count):
        row = ids_ref[t : t + 1, :].astype(F32)
        column = column_of(row)
        rank = jnp.sum(jnp.where(row < column, 1.0, 0.0), axis=1, keepdims=True).astype(jnp.int32)
        place = (rank // 2) * (2 * table_count) + 2 * t + rank % 2
        rows = slice(t * cap, (t + 1) * cap)
        order_ref[rows, :] = onehot(iota((cap, unique), 1) == place)
        local = (column.astype(jnp.int32) % run).astype(F32)
        local_ref[rows, :] = jnp.broadcast_to(local, (cap, run)).astype(BF16)
        label_ref[rows, :] = iota((cap, LANES), 0).astype(F32).astype(BF16)


def greet(barrier, dp_count, table_count):
    me_d, me_t = lax.axis_index("dp"), lax.axis_index("table")

    def signal_dp(step, carry):
        pl.semaphore_signal(barrier, inc=1, device_id={"dp": (me_d + step) % dp_count})
        return carry

    lax.fori_loop(1, dp_count, signal_dp, 0)
    for step in range(1, table_count):
        pl.semaphore_signal(barrier, inc=1, device_id={"table": (me_t + step) % table_count})


class Exchange:
    def __init__(self, axis, count, source, target, block, sems):
        self.axis, self.count, self.block = axis, count, block
        self.source, self.target = source, target
        self.send, self.recv = sems
        self.me = lax.axis_index(axis)

    def rows(self, index):
        return pl.ds(pl.multiple_of(index * self.block, self.block), self.block)

    def copy(self, peer, slot):
        return pltpu.make_async_remote_copy(
            src_ref=self.source.at[self.rows(peer)],
            dst_ref=self.target.at[self.rows(slot)],
            send_sem=self.send,
            recv_sem=self.recv,
            device_id={self.axis: peer},
        )

    def loop(self, step_fn):
        def step(index, carry):
            step_fn((self.me + index) % self.count)
            return carry

        lax.fori_loop(1, self.count, step, 0)

    def start(self):
        self.loop(lambda peer: self.copy(peer, self.me).start())
        self.target[self.rows(self.me), :] = self.source[self.rows(self.me), :]

    def wait(self, sem):
        rows = pl.ds(0, (self.count - 1) * self.block)
        pltpu.make_async_copy(self.source.at[rows], self.target.at[rows], sem).wait()

    def wait_recv(self):
        self.wait(self.recv)

    def wait_send(self):
        self.wait(self.send)


def prepare(slot_ref, labels_in, cap, here, tall, names, name_row):
    block_count, length = slot_ref.shape
    unique = here.shape[1]
    part = cap // 2
    owner = iota((unique, LANES), 0) % (unique // 2) // part
    name = labels_in[...].astype(F32) + (owner * cap).astype(F32)
    names[...] = name.astype(jnp.int32)
    name_row[...] = jnp.transpose(name)[:8, :].astype(jnp.int32)
    eye = iota((length, length), 0) == iota((length, length), 1)

    def one(b, carry):
        rows = pl.ds(pl.multiple_of(b * length, length), length)
        slot_row = slot_ref[pl.ds(b, 1), :]
        slot_col = jnp.sum(
            jnp.where(eye, slot_row.astype(F32), 0.0), axis=1, keepdims=True
        ).astype(jnp.int32)
        here[rows, :] = onehot(name_row[:1, :] == slot_col)
        tall[:, rows] = onehot(names[...] == slot_row)
        return carry

    lax.fori_loop(0, block_count, one, 0)


def weigh(fill_ref, length, w_out_ref, spread, dgated):
    events, width = dgated.shape
    cols = spread.shape[1] - width
    position = iota((length, 1), 0)

    def one(b, carry):
        rows = pl.ds(pl.multiple_of(b * length, length), length)
        aim = spread[rows, cols:]
        live_aim = jnp.where(position < fill_ref[b], aim, jnp.zeros_like(aim))
        spread[rows, cols:] = live_aim
        dgated[rows, :] = dot(live_aim, w_out_ref[...], 1, 1).astype(BF16)
        return carry

    lax.fori_loop(0, events // length, one, 0)


def project(half, rows_ref, w_in_ref, gain_in_ref, gain_out_ref, length, proj, slope, hat, inv):
    unique, width = rows_ref.shape
    unique //= 2
    query = H * QK
    gain_in = gain_in_ref[...]
    tilt = 0.5 * QK ** (-0.5)
    lane = iota((1, 2 * query), 1)
    factors = [gain_out_ref[...], 1.0 / length, jnp.where(lane < query, tilt, 1.0)]
    chunk = min(PROJECT_ROWS, unique)

    def step(i, carry):
        rows = pl.ds(pl.multiple_of(half * unique + i * chunk, chunk), chunk)
        x = rows_ref[rows, :].astype(F32)
        shifted = x - jnp.mean(x, axis=1, keepdims=True)
        scale = lax.rsqrt(jnp.mean(shifted * shifted, axis=1, keepdims=True) + EPS)
        normal = shifted * scale
        hat[rows, :] = normal
        inv[rows, :] = jnp.broadcast_to(scale, (chunk, LANES))
        normed = (normal * gain_in).astype(BF16)
        for c, factor in enumerate(factors):
            part = slice(c * width, (c + 1) * width)
            pre = dot(normed, w_in_ref[:, part])
            sig = sigmoid(pre)
            act = pre * sig
            proj[rows, part] = (act * factor).astype(BF16)
            slope[rows, part] = (sig + act * (1.0 - sig)) * factor
        return carry

    lax.fori_loop(0, unique // chunk, step, 0)


def gather(here, proj, spread):
    events = here.shape[0]
    cols = proj.shape[1]
    chunk = min(GATHER_ROWS, events)
    width = cols // 3

    def step(i, carry):
        rows = pl.ds(pl.multiple_of(i * chunk, chunk), chunk)
        for c in range(0, cols, width):
            spread[rows, c : c + width] = dot(here[rows, :], proj[:, c : c + width]).astype(BF16)
        return carry

    lax.fori_loop(0, events // chunk, step, 0)


def attend(fill_ref, length, spread, dgated, normals, last):
    events, width = dgated.shape
    query = H * QK
    cols = 2 * width + 2 * query
    head = width // H
    block_count = events // length
    group = min(BLOCK_GROUP, block_count)
    causal = iota((length, length), 0) >= iota((length, length), 1)
    key_lane = iota((length, length), 1)
    low = iota((length, LANES), 1) < QK

    def heads(x):
        zero = jnp.zeros((length, LANES), BF16)
        parts = []
        for h in range(H):
            side = h // 2
            mine = x[:, side * LANES : (side + 1) * LANES]
            mine = jnp.where(low if h % 2 == 0 else ~low, mine, zero)
            parts.append(jnp.concatenate([mine, zero] if side == 0 else [zero, mine], axis=1))
        return jnp.concatenate(parts, axis=0)

    def step(i, carry):
        blocks = [group * i + n for n in range(group)]
        rows = [pl.ds(pl.multiple_of(b * length, length), length) for b in blocks]
        fills = [fill_ref[b] for b in blocks]
        n_all = range(group)
        q4, k4, half = [], [], []
        for n in n_all:
            q = spread[rows[n], 2 * width : 2 * width + query]
            k = spread[rows[n], 2 * width + query : cols]
            q4.append(heads(q))
            k4.append(heads(k))
            half.append(dot(q4[n], k, 1, 1))
        weights, slopes, attended = [], [], []
        for n in n_all:
            seen = causal & (key_lane < fills[n])
            ws, ss, parts = [], [], []
            for h in range(H):
                s = half[n][h * length : (h + 1) * length, :]
                up = jnp.where(seen, jnp.tanh(s) + 1.0, 0.0)
                act = s * up
                ws.append(act.astype(BF16))
                ss.append(up * ((s - act) + (s + 1.0)))
                value = spread[rows[n], width + h * head : width + (h + 1) * head]
                parts.append(dot(ws[h], value))
            weights.append(ws)
            slopes.append(ss)
            attended.append(jnp.concatenate(parts, axis=1))
        shifted = [a - jnp.mean(a, axis=1, keepdims=True) for a in attended]
        scale = [lax.rsqrt(jnp.mean(a * a, axis=1, keepdims=True) + EPS) for a in shifted]
        dattended = []
        for n in n_all:
            normal = shifted[n] * scale[n]
            normals[n * length : (n + 1) * length, :] = normal
            gate = spread[rows[n], :width].astype(F32)
            upper = dgated[rows[n], :].astype(F32)
            dnormal = upper * gate
            spread[rows[n], :width] = (upper * normal).astype(BF16)
            where = jnp.maximum(fills[n] - 1, 0)
            last[pl.ds(blocks[n], 1), :] = normals[pl.ds(n * length + where, 1), :]
            mean = jnp.mean(dnormal, axis=1, keepdims=True)
            along = jnp.mean(dnormal * normal, axis=1, keepdims=True)
            dattended.append((scale[n] * (dnormal - mean - normal * along)).astype(BF16))
        dscores = []
        for n in n_all:
            ds = []
            for h in range(H):
                part = slice(h * head, (h + 1) * head)
                there = slice(width + h * head, width + (h + 1) * head)
                dweight = dot(dattended[n][:, part], spread[rows[n], there], 1, 1)
                ds.append((dweight * slopes[n][h]).astype(BF16))
                spread[rows[n], there] = dot(weights[n][h], dattended[n][:, part], 0, 0).astype(BF16)
            dscores.append(ds)
        for n in n_all:
            spread[rows[n], 2 * width : 2 * width + query] = dot(
                jnp.concatenate(dscores[n], axis=1), k4[n]
            ).astype(BF16)
            spread[rows[n], 2 * width + query : cols] = dot(
                jnp.concatenate(dscores[n], axis=0), q4[n], 0, 0
            ).astype(BF16)
        return carry

    lax.fori_loop(0, block_count // group, step, 0)


def address_letters(fills_ref, dest_ref, slot_ref, name_row, pick, chosen, flag):
    block_count, length = slot_ref.shape
    kinds = chosen.shape[0]
    fills = fills_ref[...]
    fill_col = column_of(fills.astype(F32)).astype(jnp.int32)
    last_slot = jnp.sum(
        jnp.where(iota((block_count, length), 1) == fill_col - 1, slot_ref[...].astype(F32), 0.0),
        axis=1,
        keepdims=True,
    ).astype(jnp.int32)
    pick[...] = onehot(name_row[:1, :] == last_slot)
    row = iota((flag.shape[0], block_count), 0)
    mine = (row // PACK == dest_ref[...]) & (fills > 0)
    present = jnp.sum(jnp.where(mine & (row % PACK == kinds), 1.0, 0.0), axis=1, keepdims=True)
    flag[...] = jnp.broadcast_to(present, flag.shape).astype(BF16)
    for i in range(kinds):
        chosen[i, :, :] = onehot(mine & (row % PACK == i))


def write_letters(rows_ref, w_out_ref, proj, last, pick, chosen, flag, message):
    width = rows_ref.shape[1]
    gated = (last[...] * dot(pick[...], proj[:, :width])).astype(BF16)
    summary = (dot(pick[...], rows_ref[...]) + dot(gated, w_out_ref[...])).astype(BF16)
    letter = flag[...].astype(F32)
    for i in range(chosen.shape[0]):
        letter = letter + dot(chosen[i, :, :], summary[:, i * LANES : (i + 1) * LANES])
    message[...] = letter.astype(BF16)


def read_letters(letters, summary_ref):
    rows = letters.shape[0]
    work, width = summary_ref.shape
    row, col = iota((rows, rows), 0), iota((rows, rows), 1)
    flag_col = col % PACK == width // LANES
    rank = dot(onehot(flag_col & (col // PACK < row // PACK)), letters[...])
    present = dot(onehot(flag_col & (col // PACK == row // PACK)), letters[...])
    wanted = (present > 0.5) & (rank.astype(jnp.int32) == iota((rows, LANES), 1))
    kind = iota((rows, LANES), 0) % PACK
    for i in range(width // LANES):
        part = dot(onehot(wanted & (kind == i)), letters[...], 0, 0)
        summary_ref[:, i * LANES : (i + 1) * LANES] = part[:work, :].astype(BF16)


def finish(half, w_in_ref, gain_in_ref, tall, spread, slope, hat, inv, dproj, grads):
    unique, width = hat.shape
    cols = slope.shape[1]
    tile = unique // 2
    rows = slice(half * tile, (half + 1) * tile)
    for c in range(0, cols, width):
        total = dot(tall[rows, :], spread[:, c : c + width])
        dproj[:, c : c + width] = (total * slope[rows, c : c + width]).astype(BF16)
    straight = dot(tall[rows, :], spread[:, cols:])
    dhat = dot(dproj[...], w_in_ref[...], 1, 1) * gain_in_ref[...]
    normal = hat[rows, :]
    scale = inv[rows, :1]
    mean = jnp.mean(dhat, axis=1, keepdims=True)
    along = jnp.mean(dhat * normal, axis=1, keepdims=True)
    dx = (scale * (dhat - mean - normal * along) + straight).astype(BF16)
    grads[rows, :] = dx


def step_kernel(
    dp_count,
    fill_ref, ids_ref, slot_ref, fills_ref, dest_ref, gain_in_ref, gain_out_ref,
    table_ref, aims_ref, w_in_hbm, w_out_hbm,
    summary_ref, total_ref,
    table_v, w_in_ref, w_out_ref, order, local, picks, picks_in, sorted_rows, served, rows_ref,
    here, tall, spread, dgated, proj, slope, hat, inv, normals, last, dproj,
    labels, labels_out, labels_in, shift, names, name_row, pick, chosen, flag, message, letters, grads, home, ordered, arrived,
    table_sem, load_sem, label_sems, row_sems, pick_sems, letter_sems, home_sems, total_sems,
):
    table_count, cap = ids_ref.shape
    shard_rows, width = table_ref.shape
    cols = w_in_ref.shape[1]
    unique = table_count * cap
    run = shard_rows // dp_count
    length = slot_ref.shape[1]
    group = min(8, dp_count)
    span, part = group * run, group * 2 * table_count
    loads = [
        pltpu.make_async_copy(
            table_ref.at[pl.ds(g * span, span)], table_v.at[pl.ds(g * span, span)], table_sem.at[g]
        )
        for g in range(dp_count // group)
    ]
    w_out_load = pltpu.make_async_copy(w_out_hbm, w_out_ref, load_sem.at[0])
    aims_load = pltpu.make_async_copy(
        aims_ref, spread.at[:, pl.ds(cols, width)], load_sem.at[1]
    )
    w_in_load = pltpu.make_async_copy(w_in_hbm, w_in_ref, load_sem.at[2])
    for load in loads:
        load.start()
    barrier = pltpu.get_barrier_semaphore()
    greet(barrier, dp_count, table_count)

    def pair(sems):
        return sems.at[0], sems.at[1]

    fill_order(ids_ref, order, local, labels, run)
    index = dot(order[...], local[...], 0, 0)
    picks[...] = onehot(index.astype(jnp.int32) == iota((unique, run), 1))
    shift[...] = to_halves(unique, table_count)
    placed = dot(order[...], labels[...], 0, 0).astype(BF16)
    labels_out[...] = dot(shift[...], placed).astype(BF16)
    pl.semaphore_wait(barrier, dp_count + table_count - 2)
    halves = [pl.ds(half * (unique // 2), unique // 2) for half in range(2)]
    label_exchanges = [
        Exchange(
            "table", table_count, labels_out.at[rows], labels_in.at[rows], cap // 2,
            pair(label_sems.at[half]),
        )
        for half, rows in enumerate(halves)
    ]
    for exchange in label_exchanges:
        exchange.start()
    for g, load in enumerate(loads):
        mine = picks[g * part : (g + 1) * part, :]
        wide = jnp.concatenate([mine] * group, axis=1)
        same = iota((part, span), 0) // (2 * table_count) == iota((part, span), 1) // run
        load.wait()
        if g == max(0, len(loads) - 2):
            for later in (w_out_load, aims_load, w_in_load):
                later.start()
        sorted_rows[g * part : (g + 1) * part, :] = dot(
            jnp.where(same, wide, jnp.zeros_like(wide)), table_v[g * span : (g + 1) * span, :]
        ).astype(BF16)
    served[...] = dot(shift[...], sorted_rows[...]).astype(BF16)
    row_exchanges = [
        Exchange(
            "table", table_count, served.at[rows], rows_ref.at[rows], cap // 2, pair(row_sems.at[half])
        )
        for half, rows in enumerate(halves)
    ]
    for exchange in row_exchanges:
        exchange.start()
    pick_exchange = Exchange("dp", dp_count, picks, picks_in, 2 * table_count, pair(pick_sems))
    pick_exchange.start()

    for exchange in label_exchanges:
        exchange.wait_recv()
    prepare(slot_ref, labels_in, cap, here, tall, names, name_row)
    address_letters(fills_ref, dest_ref, slot_ref, name_row, pick, chosen, flag)
    w_out_load.wait()
    aims_load.wait()
    weigh(fill_ref, length, w_out_ref, spread, dgated)
    w_in_load.wait()
    for half, exchange in enumerate(row_exchanges):
        exchange.wait_recv()
        project(
            half, rows_ref, w_in_ref, gain_in_ref, gain_out_ref, length, proj, slope, hat, inv
        )
    gather(here, proj, spread)
    attend(fill_ref, length, spread, dgated, normals, last)
    write_letters(rows_ref, w_out_ref, proj, last, pick, chosen, flag, message)

    pack = 2 * table_count
    me = lax.axis_index("dp")
    letter_exchange = Exchange("dp", dp_count, message, letters, PACK, pair(letter_sems))
    total_exchange = Exchange("dp", dp_count, ordered, arrived, pack, pair(total_sems))

    def send_totals(half):
        there = halves[half]
        ordered[there, :] = dot(from_half(unique // 2, table_count), home[there, :]).astype(BF16)

        def send(index, carry):
            place = (me // 2 + index) % (dp_count // 2)
            peer = 2 * place + half
            source = ordered.at[
                pl.ds(pl.multiple_of(half * (unique // 2) + place * pack, pack), pack)
            ]
            target = arrived.at[total_exchange.rows(me)]

            @pl.when(peer != me)
            def _():
                pltpu.make_async_remote_copy(
                    src_ref=source,
                    dst_ref=target,
                    send_sem=total_exchange.send,
                    recv_sem=total_exchange.recv,
                    device_id={"dp": peer},
                ).start()

            @pl.when(peer == me)
            def _():
                target[...] = source[...]

            return carry

        lax.fori_loop(0, dp_count // 2, send, 0)

    homes = []
    for half, rows in enumerate(halves):
        finish(half, w_in_ref, gain_in_ref, tall, spread, slope, hat, inv, dproj, grads)
        home_exchange = Exchange(
            "table", table_count, grads.at[rows], home.at[rows], cap // 2, pair(home_sems.at[half])
        )
        home_exchange.start()
        homes.append(home_exchange)
        if half == 0:
            letter_exchange.start()
    for half in range(2):
        homes[half].wait_recv()
        send_totals(half)
    letter_exchange.wait_recv()
    read_letters(letters, summary_ref)
    pick_exchange.wait_recv()
    for exchange in label_exchanges + row_exchanges + [pick_exchange, letter_exchange] + homes:
        exchange.wait_send()
    total_exchange.wait_recv()
    total_ref[...] = dot(picks_in[...], arrived[...], 0, 0)
    total_exchange.wait_send()


def hand_on(summary_in, total_in, summary_out, total_out):
    summary_out[...] = summary_in[...]
    total_out[...] = total_in[...]


def whole(space=pltpu.VMEM):
    return pl.BlockSpec(memory_space=space)


def body(
    embedding_table, served_ids, event_slot, block_fill, destination, target, w_in, w_out,
    gain_in, gain_out,
):
    dp_count, table_count = lax.axis_size("dp"), lax.axis_size("table")
    shard_rows, width = embedding_table.shape
    ids = served_ids[0, 0]
    cap = ids.shape[1]
    unique = table_count * cap
    run = shard_rows // dp_count
    slots = event_slot[0, 0]
    block_count, length = slots.shape
    work_count = block_count // 2
    events = block_count * length
    cols = w_in.shape[1]
    dma = pltpu.SemaphoreType.DMA
    vmem = pltpu.VMEM
    fills = block_fill[0, 0]
    summary, total = pl.pallas_call(
        functools.partial(step_kernel, dp_count),
        out_shape=(
            jax.ShapeDtypeStruct((work_count, width), BF16),
            jax.ShapeDtypeStruct((run, width), F32),
        ),
        in_specs=[whole(pltpu.SMEM)] + [whole()] * 6 + [whole(pl.ANY)] * 4,
        out_specs=(whole(), whole()),
        scratch_shapes=[
            vmem((shard_rows, width), BF16),
            vmem((width, cols), BF16),
            vmem((width, width), BF16),
            vmem((unique, unique), BF16),
            vmem((unique, run), BF16),
            vmem((unique, run), BF16),
            vmem((unique, run), BF16),
            vmem((unique, width), BF16),
            vmem((unique, width), BF16),
            vmem((unique, width), BF16),
        ]
        + compute_scratch(unique, events, cols, width, block_count, length)
        + [
            vmem((unique, LANES), BF16),
            vmem((unique, LANES), BF16),
            vmem((unique, LANES), BF16),
            vmem((unique, unique), BF16),
            vmem((unique, LANES), jnp.int32),
            vmem((8, unique), jnp.int32),
            vmem((block_count, unique), BF16),
            vmem((width // LANES, dp_count * PACK, block_count), BF16),
            vmem((dp_count * PACK, LANES), BF16),
            vmem((dp_count * PACK, LANES), BF16),
            vmem((dp_count * PACK, LANES), BF16),
            vmem((unique, width), BF16),
            vmem((unique, width), BF16),
            vmem((unique, width), BF16),
            vmem((unique, width), BF16),
            dma((max(1, dp_count // 8),)),
            dma((3,)),
            dma((2, 2)),
            dma((2, 2)),
            dma((2,)),
            dma((2,)),
            dma((2, 2)),
            dma((2,)),
        ],
        compiler_params=pltpu.CompilerParams(
            vmem_limit_bytes=VMEM_BYTES, collective_id=0, has_side_effects=True
        ),
        name="step",
    )(
        fills, ids, slots, fills.reshape(1, -1), destination[0, 0].reshape(1, -1),
        gain_in.reshape(1, -1), gain_out.reshape(1, -1),
        embedding_table, target.reshape(events, width), w_in, w_out,
    )
    summary, total = pl.pallas_call(
        hand_on,
        out_shape=(
            jax.ShapeDtypeStruct((work_count, width), BF16),
            jax.ShapeDtypeStruct((run, width), F32),
        ),
        in_specs=[whole()] * 2,
        out_specs=(whole(), whole()),
        compiler_params=pltpu.CompilerParams(vmem_limit_bytes=VMEM_BYTES),
        name="hand_on",
    )(summary, total)
    return (summary.reshape(1, 1, work_count, width), total.reshape(1, run, width))


def compute_scratch(unique, events, cols, width, block_count, length):
    vmem = pltpu.VMEM
    return [
        vmem((events, unique), BF16),
        vmem((unique, events), BF16),
        vmem((events, cols + width), BF16),
        vmem((events, width), BF16),
        vmem((unique, cols), BF16),
        vmem((unique, cols), F32),
        vmem((unique, width), F32),
        vmem((unique, LANES), F32),
        vmem((BLOCK_GROUP * length, width), F32),
        vmem((block_count, width), F32),
        vmem((unique // 2, cols), BF16),
    ]


def solution(mesh):
    return jax.shard_map(
        body,
        mesh=mesh,
        in_specs=(
            P("table", None),
            P("dp", "table", None, None),
            P("dp", "table", None, None),
            P("dp", "table", None),
            P("dp", "table", None),
            P("dp", "table", None, None, None),
            P(), P(), P(), P(),
        ),
        out_specs=(P("dp", "table", None, None), P("table", "dp", None)),
        check_vma=False,
    )
```

```python
import functools

import jax
import jax.numpy as jnp
from jax import lax
from jax.experimental import pallas as pl
from jax.experimental.pallas import tpu as pltpu
from jax.sharding import PartitionSpec as P

H = 4
QK = 64
PACK = 16
LANES = 128
EPS = 1e-05
F32 = jnp.float32
BF16 = jnp.bfloat16
VMEM_BYTES = 60 * 1024 * 1024
PROJECT_ROWS = 256
GATHER_ROWS = 1024
BLOCK_GROUP = 8


def dot(a, b, ca=1, cb=0):
    return lax.dot_general(a, b, (((ca,), (cb,)), ((), ())), preferred_element_type=F32)


def iota(shape, axis):
    return lax.broadcasted_iota(jnp.int32, shape, axis)


def onehot(condition):
    return jnp.where(condition, 1.0, 0.0).astype(BF16)


def sigmoid(x):
    return 0.5 * jnp.tanh(0.5 * x) + 0.5


def column_of(row):
    n = row.shape[1]
    here = iota((n, n), 0) == iota((n, n), 1)
    return jnp.sum(jnp.where(here, row, 0.0), axis=1, keepdims=True)


def to_halves(unique, table_count):
    part = unique // 2 // table_count
    row, col = iota((unique, unique), 0), iota((unique, unique), 1)
    half, t, place = row // (unique // 2), row // part % table_count, row % part
    return onehot(col == (place // 2 * 2 + half) * (2 * table_count) + 2 * t + place % 2)


def from_half(size, table_count):
    row, col = iota((size, size), 0), iota((size, size), 1)
    pack = 2 * table_count
    return onehot(col == row % pack // 2 * (size // table_count) + row // pack * 2 + row % 2)


def fill_order(ids_ref, order_ref, local_ref, label_ref, run):
    table_count, cap = ids_ref.shape
    unique = table_count * cap
    for t in range(table_count):
        row = ids_ref[t : t + 1, :].astype(F32)
        column = column_of(row)
        rank = jnp.sum(jnp.where(row < column, 1.0, 0.0), axis=1, keepdims=True).astype(jnp.int32)
        place = (rank // 2) * (2 * table_count) + 2 * t + rank % 2
        rows = slice(t * cap, (t + 1) * cap)
        order_ref[rows, :] = onehot(iota((cap, unique), 1) == place)
        local = (column.astype(jnp.int32) % run).astype(F32)
        local_ref[rows, :] = jnp.broadcast_to(local, (cap, run)).astype(BF16)
        label_ref[rows, :] = iota((cap, LANES), 0).astype(F32).astype(BF16)


def greet(barrier, dp_count, table_count):
    me_d, me_t = lax.axis_index("dp"), lax.axis_index("table")

    def signal_dp(step, carry):
        pl.semaphore_signal(barrier, inc=1, device_id={"dp": (me_d + step) % dp_count})
        return carry

    lax.fori_loop(1, dp_count, signal_dp, 0)
    for step in range(1, table_count):
        pl.semaphore_signal(barrier, inc=1, device_id={"table": (me_t + step) % table_count})


class Exchange:
    def __init__(self, axis, count, source, target, block, sems):
        self.axis, self.count, self.block = axis, count, block
        self.source, self.target = source, target
        self.send, self.recv = sems
        self.me = lax.axis_index(axis)

    def rows(self, index):
        return pl.ds(pl.multiple_of(index * self.block, self.block), self.block)

    def copy(self, peer, slot):
        return pltpu.make_async_remote_copy(
            src_ref=self.source.at[self.rows(peer)],
            dst_ref=self.target.at[self.rows(slot)],
            send_sem=self.send,
            recv_sem=self.recv,
            device_id={self.axis: peer},
        )

    def loop(self, step_fn):
        def step(index, carry):
            step_fn((self.me + index) % self.count)
            return carry

        lax.fori_loop(1, self.count, step, 0)

    def start(self):
        self.loop(lambda peer: self.copy(peer, self.me).start())
        self.target[self.rows(self.me), :] = self.source[self.rows(self.me), :]

    def wait(self, sem):
        rows = pl.ds(0, (self.count - 1) * self.block)
        pltpu.make_async_copy(self.source.at[rows], self.target.at[rows], sem).wait()

    def wait_recv(self):
        self.wait(self.recv)

    def wait_send(self):
        self.wait(self.send)


def prepare(slot_ref, labels_in, cap, here, tall, names, name_row):
    block_count, length = slot_ref.shape
    unique = here.shape[1]
    part = cap // 2
    owner = iota((unique, LANES), 0) % (unique // 2) // part
    name = labels_in[...].astype(F32) + (owner * cap).astype(F32)
    names[...] = name.astype(jnp.int32)
    name_row[...] = jnp.transpose(name)[:8, :].astype(jnp.int32)
    eye = iota((length, length), 0) == iota((length, length), 1)

    def one(b, carry):
        rows = pl.ds(pl.multiple_of(b * length, length), length)
        slot_row = slot_ref[pl.ds(b, 1), :]
        slot_col = jnp.sum(
            jnp.where(eye, slot_row.astype(F32), 0.0), axis=1, keepdims=True
        ).astype(jnp.int32)
        here[rows, :] = onehot(name_row[:1, :] == slot_col)
        tall[:, rows] = onehot(names[...] == slot_row)
        return carry

    lax.fori_loop(0, block_count, one, 0)


def weigh(fill_ref, length, w_out_ref, spread, dgated):
    events, width = dgated.shape
    cols = spread.shape[1] - width
    position = iota((length, 1), 0)

    def one(b, carry):
        rows = pl.ds(pl.multiple_of(b * length, length), length)
        aim = spread[rows, cols:]
        live_aim = jnp.where(position < fill_ref[b], aim, jnp.zeros_like(aim))
        spread[rows, cols:] = live_aim
        dgated[rows, :] = dot(live_aim, w_out_ref[...], 1, 1).astype(BF16)
        return carry

    lax.fori_loop(0, events // length, one, 0)


def project(half, rows_ref, w_in_ref, gain_in_ref, gain_out_ref, length, proj, slope, hat, inv):
    unique, width = rows_ref.shape
    unique //= 2
    query = H * QK
    gain_in = gain_in_ref[...]
    tilt = 0.5 * QK ** (-0.5)
    lane = iota((1, 2 * query), 1)
    factors = [gain_out_ref[...], 1.0 / length, jnp.where(lane < query, tilt, 1.0)]
    chunk = min(PROJECT_ROWS, unique)

    def step(i, carry):
        rows = pl.ds(pl.multiple_of(half * unique + i * chunk, chunk), chunk)
        x = rows_ref[rows, :].astype(F32)
        shifted = x - jnp.mean(x, axis=1, keepdims=True)
        scale = lax.rsqrt(jnp.mean(shifted * shifted, axis=1, keepdims=True) + EPS)
        normal = shifted * scale
        hat[rows, :] = normal
        inv[rows, :] = jnp.broadcast_to(scale, (chunk, LANES))
        normed = (normal * gain_in).astype(BF16)
        for c, factor in enumerate(factors):
            part = slice(c * width, (c + 1) * width)
            pre = dot(normed, w_in_ref[:, part])
            sig = sigmoid(pre)
            act = pre * sig
            proj[rows, part] = (act * factor).astype(BF16)
            slope[rows, part] = (sig + act * (1.0 - sig)) * factor
        return carry

    lax.fori_loop(0, unique // chunk, step, 0)


def gather(here, proj, spread):
    events = here.shape[0]
    cols = proj.shape[1]
    chunk = min(GATHER_ROWS, events)
    width = cols // 3

    def step(i, carry):
        rows = pl.ds(pl.multiple_of(i * chunk, chunk), chunk)
        for c in range(0, cols, width):
            spread[rows, c : c + width] = dot(here[rows, :], proj[:, c : c + width]).astype(BF16)
        return carry

    lax.fori_loop(0, events // chunk, step, 0)


def attend(fill_ref, length, spread, dgated, normals, last):
    events, width = dgated.shape
    query = H * QK
    cols = 2 * width + 2 * query
    head = width // H
    block_count = events // length
    group = min(BLOCK_GROUP, block_count)
    causal = iota((length, length), 0) >= iota((length, length), 1)
    key_lane = iota((length, length), 1)
    low = iota((length, LANES), 1) < QK

    def heads(x):
        zero = jnp.zeros((length, LANES), BF16)
        parts = []
        for h in range(H):
            side = h // 2
            mine = x[:, side * LANES : (side + 1) * LANES]
            mine = jnp.where(low if h % 2 == 0 else ~low, mine, zero)
            parts.append(jnp.concatenate([mine, zero] if side == 0 else [zero, mine], axis=1))
        return jnp.concatenate(parts, axis=0)

    def step(i, carry):
        blocks = [group * i + n for n in range(group)]
        rows = [pl.ds(pl.multiple_of(b * length, length), length) for b in blocks]
        fills = [fill_ref[b] for b in blocks]
        n_all = range(group)
        q4, k4, half = [], [], []
        for n in n_all:
            q = spread[rows[n], 2 * width : 2 * width + query]
            k = spread[rows[n], 2 * width + query : cols]
            q4.append(heads(q))
            k4.append(heads(k))
            half.append(dot(q4[n], k, 1, 1))
        weights, slopes, attended = [], [], []
        for n in n_all:
            seen = causal & (key_lane < fills[n])
            ws, ss, parts = [], [], []
            for h in range(H):
                s = half[n][h * length : (h + 1) * length, :]
                up = jnp.where(seen, jnp.tanh(s) + 1.0, 0.0)
                act = s * up
                ws.append(act.astype(BF16))
                ss.append(up * ((s - act) + (s + 1.0)))
                value = spread[rows[n], width + h * head : width + (h + 1) * head]
                parts.append(dot(ws[h], value))
            weights.append(ws)
            slopes.append(ss)
            attended.append(jnp.concatenate(parts, axis=1))
        shifted = [a - jnp.mean(a, axis=1, keepdims=True) for a in attended]
        scale = [lax.rsqrt(jnp.mean(a * a, axis=1, keepdims=True) + EPS) for a in shifted]
        dattended = []
        for n in n_all:
            normal = shifted[n] * scale[n]
            normals[n * length : (n + 1) * length, :] = normal
            gate = spread[rows[n], :width].astype(F32)
            upper = dgated[rows[n], :].astype(F32)
            dnormal = upper * gate
            spread[rows[n], :width] = (upper * normal).astype(BF16)
            where = jnp.maximum(fills[n] - 1, 0)
            last[pl.ds(blocks[n], 1), :] = normals[pl.ds(n * length + where, 1), :]
            mean = jnp.mean(dnormal, axis=1, keepdims=True)
            along = jnp.mean(dnormal * normal, axis=1, keepdims=True)
            dattended.append((scale[n] * (dnormal - mean - normal * along)).astype(BF16))
        dscores = []
        for n in n_all:
            ds = []
            for h in range(H):
                part = slice(h * head, (h + 1) * head)
                there = slice(width + h * head, width + (h + 1) * head)
                dweight = dot(dattended[n][:, part], spread[rows[n], there], 1, 1)
                ds.append((dweight * slopes[n][h]).astype(BF16))
                spread[rows[n], there] = dot(weights[n][h], dattended[n][:, part], 0, 0).astype(BF16)
            dscores.append(ds)
        for n in n_all:
            spread[rows[n], 2 * width : 2 * width + query] = dot(
                jnp.concatenate(dscores[n], axis=1), k4[n]
            ).astype(BF16)
            spread[rows[n], 2 * width + query : cols] = dot(
                jnp.concatenate(dscores[n], axis=0), q4[n], 0, 0
            ).astype(BF16)
        return carry

    lax.fori_loop(0, block_count // group, step, 0)


def address_letters(fills_ref, dest_ref, slot_ref, name_row, pick, chosen, flag):
    block_count, length = slot_ref.shape
    kinds = chosen.shape[0]
    fills = fills_ref[...]
    fill_col = column_of(fills.astype(F32)).astype(jnp.int32)
    last_slot = jnp.sum(
        jnp.where(iota((block_count, length), 1) == fill_col - 1, slot_ref[...].astype(F32), 0.0),
        axis=1,
        keepdims=True,
    ).astype(jnp.int32)
    pick[...] = onehot(name_row[:1, :] == last_slot)
    row = iota((flag.shape[0], block_count), 0)
    mine = (row // PACK == dest_ref[...]) & (fills > 0)
    present = jnp.sum(jnp.where(mine & (row % PACK == kinds), 1.0, 0.0), axis=1, keepdims=True)
    flag[...] = jnp.broadcast_to(present, flag.shape).astype(BF16)
    for i in range(kinds):
        chosen[i, :, :] = onehot(mine & (row % PACK == i))


def write_letters(rows_ref, w_out_ref, proj, last, pick, chosen, flag, message):
    width = rows_ref.shape[1]
    gated = (last[...] * dot(pick[...], proj[:, :width])).astype(BF16)
    summary = (dot(pick[...], rows_ref[...]) + dot(gated, w_out_ref[...])).astype(BF16)
    letter = flag[...].astype(F32)
    for i in range(chosen.shape[0]):
        letter = letter + dot(chosen[i, :, :], summary[:, i * LANES : (i + 1) * LANES])
    message[...] = letter.astype(BF16)


def read_letters(letters, summary_ref):
    rows = letters.shape[0]
    work, width = summary_ref.shape
    row, col = iota((rows, rows), 0), iota((rows, rows), 1)
    flag_col = col % PACK == width // LANES
    rank = dot(onehot(flag_col & (col // PACK < row // PACK)), letters[...])
    present = dot(onehot(flag_col & (col // PACK == row // PACK)), letters[...])
    wanted = (present > 0.5) & (rank.astype(jnp.int32) == iota((rows, LANES), 1))
    kind = iota((rows, LANES), 0) % PACK
    for i in range(width // LANES):
        part = dot(onehot(wanted & (kind == i)), letters[...], 0, 0)
        summary_ref[:, i * LANES : (i + 1) * LANES] = part[:work, :].astype(BF16)


def finish(half, w_in_ref, gain_in_ref, tall, spread, slope, hat, inv, dproj, grads):
    unique, width = hat.shape
    cols = slope.shape[1]
    tile = unique // 2
    rows = slice(half * tile, (half + 1) * tile)
    for c in range(0, cols, width):
        total = dot(tall[rows, :], spread[:, c : c + width])
        dproj[:, c : c + width] = (total * slope[rows, c : c + width]).astype(BF16)
    straight = dot(tall[rows, :], spread[:, cols:])
    dhat = dot(dproj[...], w_in_ref[...], 1, 1) * gain_in_ref[...]
    normal = hat[rows, :]
    scale = inv[rows, :1]
    mean = jnp.mean(dhat, axis=1, keepdims=True)
    along = jnp.mean(dhat * normal, axis=1, keepdims=True)
    dx = (scale * (dhat - mean - normal * along) + straight).astype(BF16)
    grads[rows, :] = dx


def step_kernel(
    dp_count,
    fill_ref, ids_ref, slot_ref, fills_ref, dest_ref, gain_in_ref, gain_out_ref,
    table_ref, aims_ref, w_in_hbm, w_out_hbm,
    summary_ref, total_ref,
    table_v, w_in_ref, w_out_ref, order, local, picks, picks_in, sorted_rows, served, rows_ref,
    here, tall, spread, dgated, proj, slope, hat, inv, normals, last, dproj,
    labels, labels_out, labels_in, shift, names, name_row, pick, chosen, flag, message, letters, grads, home, ordered, arrived,
    table_sem, load_sem, label_sems, row_sems, pick_sems, letter_sems, home_sems, total_sems,
):
    table_count, cap = ids_ref.shape
    shard_rows, width = table_ref.shape
    cols = w_in_ref.shape[1]
    unique = table_count * cap
    run = shard_rows // dp_count
    length = slot_ref.shape[1]
    group = min(8, dp_count)
    span, part = group * run, group * 2 * table_count
    loads = [
        pltpu.make_async_copy(
            table_ref.at[pl.ds(g * span, span)], table_v.at[pl.ds(g * span, span)], table_sem.at[g]
        )
        for g in range(dp_count // group)
    ]
    w_out_load = pltpu.make_async_copy(w_out_hbm, w_out_ref, load_sem.at[0])
    aims_load = pltpu.make_async_copy(
        aims_ref, spread.at[:, pl.ds(cols, width)], load_sem.at[1]
    )
    w_in_load = pltpu.make_async_copy(w_in_hbm, w_in_ref, load_sem.at[2])
    for load in loads:
        load.start()
    barrier = pltpu.get_barrier_semaphore()
    greet(barrier, dp_count, table_count)

    def pair(sems):
        return sems.at[0], sems.at[1]

    fill_order(ids_ref, order, local, labels, run)
    index = dot(order[...], local[...], 0, 0)
    picks[...] = onehot(index.astype(jnp.int32) == iota((unique, run), 1))
    shift[...] = to_halves(unique, table_count)
    placed = dot(order[...], labels[...], 0, 0).astype(BF16)
    labels_out[...] = dot(shift[...], placed).astype(BF16)
    pl.semaphore_wait(barrier, dp_count + table_count - 2)
    halves = [pl.ds(half * (unique // 2), unique // 2) for half in range(2)]
    label_exchanges = [
        Exchange(
            "table", table_count, labels_out.at[rows], labels_in.at[rows], cap // 2,
            pair(label_sems.at[half]),
        )
        for half, rows in enumerate(halves)
    ]
    for exchange in label_exchanges:
        exchange.start()
    for g, load in enumerate(loads):
        mine = picks[g * part : (g + 1) * part, :]
        wide = jnp.concatenate([mine] * group, axis=1)
        same = iota((part, span), 0) // (2 * table_count) == iota((part, span), 1) // run
        load.wait()
        if g == max(0, len(loads) - 2):
            for later in (w_out_load, aims_load, w_in_load):
                later.start()
        sorted_rows[g * part : (g + 1) * part, :] = dot(
            jnp.where(same, wide, jnp.zeros_like(wide)), table_v[g * span : (g + 1) * span, :]
        ).astype(BF16)
    served[...] = dot(shift[...], sorted_rows[...]).astype(BF16)
    row_exchanges = [
        Exchange(
            "table", table_count, served.at[rows], rows_ref.at[rows], cap // 2, pair(row_sems.at[half])
        )
        for half, rows in enumerate(halves)
    ]
    for exchange in row_exchanges:
        exchange.start()
    pick_exchange = Exchange("dp", dp_count, picks, picks_in, 2 * table_count, pair(pick_sems))
    pick_exchange.start()

    for exchange in label_exchanges:
        exchange.wait_recv()
    prepare(slot_ref, labels_in, cap, here, tall, names, name_row)
    address_letters(fills_ref, dest_ref, slot_ref, name_row, pick, chosen, flag)
    w_out_load.wait()
    aims_load.wait()
    weigh(fill_ref, length, w_out_ref, spread, dgated)
    w_in_load.wait()
    for half, exchange in enumerate(row_exchanges):
        exchange.wait_recv()
        project(
            half, rows_ref, w_in_ref, gain_in_ref, gain_out_ref, length, proj, slope, hat, inv
        )
    gather(here, proj, spread)
    attend(fill_ref, length, spread, dgated, normals, last)
    write_letters(rows_ref, w_out_ref, proj, last, pick, chosen, flag, message)

    pack = 2 * table_count
    me = lax.axis_index("dp")
    letter_exchange = Exchange("dp", dp_count, message, letters, PACK, pair(letter_sems))
    total_exchange = Exchange("dp", dp_count, ordered, arrived, pack, pair(total_sems))

    def send_totals(half):
        there = halves[half]
        ordered[there, :] = dot(from_half(unique // 2, table_count), home[there, :]).astype(BF16)

        def send(index, carry):
            place = (me // 2 + index) % (dp_count // 2)
            peer = 2 * place + half
            source = ordered.at[
                pl.ds(pl.multiple_of(half * (unique // 2) + place * pack, pack), pack)
            ]
            target = arrived.at[total_exchange.rows(me)]

            @pl.when(peer != me)
            def _():
                pltpu.make_async_remote_copy(
                    src_ref=source,
                    dst_ref=target,
                    send_sem=total_exchange.send,
                    recv_sem=total_exchange.recv,
                    device_id={"dp": peer},
                ).start()

            @pl.when(peer == me)
            def _():
                target[...] = source[...]

            return carry

        lax.fori_loop(0, dp_count // 2, send, 0)

    homes = []
    for half, rows in enumerate(halves):
        finish(half, w_in_ref, gain_in_ref, tall, spread, slope, hat, inv, dproj, grads)
        home_exchange = Exchange(
            "table", table_count, grads.at[rows], home.at[rows], cap // 2, pair(home_sems.at[half])
        )
        home_exchange.start()
        homes.append(home_exchange)
        if half == 0:
            letter_exchange.start()
    for half in range(2):
        homes[half].wait_recv()
        send_totals(half)
    letter_exchange.wait_recv()
    read_letters(letters, summary_ref)
    pick_exchange.wait_recv()
    for exchange in label_exchanges + row_exchanges + [pick_exchange, letter_exchange] + homes:
        exchange.wait_send()
    total_exchange.wait_recv()
    total_ref[...] = dot(picks_in[...], arrived[...], 0, 0)
    total_exchange.wait_send()


def hand_on(summary_in, total_in, summary_out, total_out):
    summary_out[...] = summary_in[...]
    total_out[...] = total_in[...]


def whole(space=pltpu.VMEM):
    return pl.BlockSpec(memory_space=space)


def body(
    embedding_table, served_ids, event_slot, block_fill, destination, target, w_in, w_out,
    gain_in, gain_out,
):
    dp_count, table_count = lax.axis_size("dp"), lax.axis_size("table")
    shard_rows, width = embedding_table.shape
    ids = served_ids[0, 0]
    cap = ids.shape[1]
    unique = table_count * cap
    run = shard_rows // dp_count
    slots = event_slot[0, 0]
    block_count, length = slots.shape
    work_count = block_count // 2
    events = block_count * length
    cols = w_in.shape[1]
    dma = pltpu.SemaphoreType.DMA
    vmem = pltpu.VMEM
    fills = block_fill[0, 0]
    summary, total = pl.pallas_call(
        functools.partial(step_kernel, dp_count),
        out_shape=(
            jax.ShapeDtypeStruct((work_count, width), BF16),
            jax.ShapeDtypeStruct((run, width), F32),
        ),
        in_specs=[whole(pltpu.SMEM)] + [whole()] * 6 + [whole(pl.ANY)] * 4,
        out_specs=(whole(), whole()),
        scratch_shapes=[
            vmem((shard_rows, width), BF16),
            vmem((width, cols), BF16),
            vmem((width, width), BF16),
            vmem((unique, unique), BF16),
            vmem((unique, run), BF16),
            vmem((unique, run), BF16),
            vmem((unique, run), BF16),
            vmem((unique, width), BF16),
            vmem((unique, width), BF16),
            vmem((unique, width), BF16),
        ]
        + compute_scratch(unique, events, cols, width, block_count, length)
        + [
            vmem((unique, LANES), BF16),
            vmem((unique, LANES), BF16),
            vmem((unique, LANES), BF16),
            vmem((unique, unique), BF16),
            vmem((unique, LANES), jnp.int32),
            vmem((8, unique), jnp.int32),
            vmem((block_count, unique), BF16),
            vmem((width // LANES, dp_count * PACK, block_count), BF16),
            vmem((dp_count * PACK, LANES), BF16),
            vmem((dp_count * PACK, LANES), BF16),
            vmem((dp_count * PACK, LANES), BF16),
            vmem((unique, width), BF16),
            vmem((unique, width), BF16),
            vmem((unique, width), BF16),
            vmem((unique, width), BF16),
            dma((max(1, dp_count // 8),)),
            dma((3,)),
            dma((2, 2)),
            dma((2, 2)),
            dma((2,)),
            dma((2,)),
            dma((2, 2)),
            dma((2,)),
        ],
        compiler_params=pltpu.CompilerParams(
            vmem_limit_bytes=VMEM_BYTES, collective_id=0, has_side_effects=True
        ),
        name="step",
    )(
        fills, ids, slots, fills.reshape(1, -1), destination[0, 0].reshape(1, -1),
        gain_in.reshape(1, -1), gain_out.reshape(1, -1),
        embedding_table, target.reshape(events, width), w_in, w_out,
    )
    summary, total = pl.pallas_call(
        hand_on,
        out_shape=(
            jax.ShapeDtypeStruct((work_count, width), BF16),
            jax.ShapeDtypeStruct((run, width), F32),
        ),
        in_specs=[whole()] * 2,
        out_specs=(whole(), whole()),
        compiler_params=pltpu.CompilerParams(vmem_limit_bytes=VMEM_BYTES),
        name="hand_on",
    )(summary, total)
    return (summary.reshape(1, 1, work_count, width), total.reshape(1, run, width))


def compute_scratch(unique, events, cols, width, block_count, length):
    vmem = pltpu.VMEM
    return [
        vmem((events, unique), BF16),
        vmem((unique, events), BF16),
        vmem((events, cols + width), BF16),
        vmem((events, width), BF16),
        vmem((unique, cols), BF16),
        vmem((unique, cols), F32),
        vmem((unique, width), F32),
        vmem((unique, LANES), F32),
        vmem((BLOCK_GROUP * length, width), F32),
        vmem((block_count, width), F32),
        vmem((unique // 2, cols), BF16),
    ]


def solution(mesh):
    return jax.shard_map(
        body,
        mesh=mesh,
        in_specs=(
            P("table", None),
            P("dp", "table", None, None),
            P("dp", "table", None, None),
            P("dp", "table", None),
            P("dp", "table", None),
            P("dp", "table", None, None, None),
            P(), P(), P(), P(),
        ),
        out_specs=(P("dp", "table", None, None), P("table", "dp", None)),
        check_vma=False,
    )
```
